128 devices in a mesh: group: 32 (over y, x, core), blk: 4 (over z).
Axes of the slice: x: 4, y: 4, z: 4, core: 2. Of those that a mesh axis runs over, the one named last changes fastest.
Arguments:
- inverses: bfloat16 [8, 1536, 1536], P('blk', 'group'), may hold values from -0.5 to 2
- lower: bfloat16 [8, 1536, 1536], P('blk', 'group'), may hold values from -0.5 to 0.5
- forcing: bfloat16 [8, 1536, 32], P('blk', 'group'), may hold values from -1.796875 to 1.796875
- inflow: float32 [1536, 32], P('group'), may hold values from -6 to 6
Outputs:
- states: float32 [8, 1536, 32], P('blk', 'group')
The draws below stay inside these ranges and needn't reach their ends.
All inputs are finite; a program needn't handle non-finite values.
Results may differ from the reference program's by a relative error of at most 0.0057.
Values may be sent and summed in bfloat16 or wider, within the bound.
No kernel may reach another device: no remote copies, remote signals or barrier semaphores. Data moves between devices by JAX's collectives and lax.ppermute only.
A program may use at most 64 MiB of HBM per device.

```python
import jax
import jax.numpy as jnp
from jax import lax

NB = 1536
R = 32
STATIONS = 8


def draw_inverses(key, part):
    first, second = jax.random.split(jax.random.fold_in(key, 11))
    diagonal = jnp.exp(jax.random.uniform(first, (STATIONS, NB), jnp.float32, -0.35, 0.35))
    noise = jax.random.truncated_normal(second, -4.0, 4.0, (STATIONS, NB, NB), jnp.float32)
    identity = jnp.eye(NB, dtype=jnp.float32)
    return (identity[None, :, :] * diagonal[:, :, None] + 0.35 * noise / NB ** 0.5).astype(jnp.bfloat16)


def draw_lower(key, part):
    noise_key = jax.random.fold_in(key, 23)
    noise = jax.random.truncated_normal(noise_key, -4.0, 4.0, (STATIONS, NB, NB), jnp.float32)
    return (0.92 * noise / NB ** 0.5).astype(jnp.bfloat16)


def block_scale(own_key, dims, cuts, least, top_value):
    level = 1.0
    for position, shards_of in cuts:
        steps = jax.random.uniform(jax.random.fold_in(jax.random.fold_in(own_key, 6), position), (shards_of,), jnp.float32, least / len(cuts), top_value / len(cuts))
        level = level * jnp.repeat(jnp.exp(steps), dims[position] // shards_of).reshape((-1,) + (1,) * (len(dims) - 1 - position))
    return level


def gaussian(stream_key, shape, width, most, cuts=(), kind=jnp.bfloat16):
    factor_of = block_scale(stream_key, shape, cuts, -0.22, 0.18) if cuts else 1.0
    entries = jax.random.normal(stream_key, shape, jnp.float32) * width * factor_of
    return jnp.minimum(jnp.maximum(entries, -most), most).astype(kind)


def setup_inputs(seed: int = 0) -> dict:
    seeds = jax.random.split(jax.random.key(seed), 5)
    inverses = draw_inverses(jax.random.fold_in(seeds[4], 71), 0)
    lower = draw_lower(jax.random.fold_in(seeds[4], 71), 0)
    forcing = gaussian(seeds[2], (STATIONS, NB, R), 0.3, 1.796875, ((0, 4), (1, 32)))
    inflow = gaussian(seeds[3], (NB, R), 1.0, 6.0, ((0, 32),), jnp.float32)
    return {"inverses": inverses, "lower": lower, "forcing": forcing, "inflow": inflow}


def reference(inverses, lower, forcing, inflow):
    def station(state, blocks):
        inverse_block, lower_block, rhs_block = blocks
        coupling = jnp.dot(inverse_block, lower_block, preferred_element_type=jnp.float32).astype(jnp.bfloat16)
        local = jnp.dot(inverse_block, rhs_block, preferred_element_type=jnp.float32)
        fresh = local - jnp.dot(coupling, state, preferred_element_type=jnp.float32, precision=lax.Precision.HIGHEST)
        return fresh, fresh

    final_state, states = lax.scan(station, inflow, (inverses, lower, forcing))
    return states
```

```python
import jax
import jax.numpy as jnp
from jax import lax
from jax.sharding import PartitionSpec as P

Y, X, CORES, Z = 4, 4, 2, 4
AXES = ("group", "blk")
HIGHEST = lax.Precision.HIGHEST


def send(value, target):
    pairs = []
    for y in range(Y):
        for x in range(X):
            for c in range(CORES):
                for z in range(Z):
                    to = target(y, x, c, z)
                    if to is not None:
                        ty, tx, tc, tz = to
                        pairs.append((
                            ((y * X + x) * CORES + c) * Z + z,
                            ((ty * X + tx) * CORES + tc) * Z + tz,
                        ))
    return lax.ppermute(value, AXES, pairs)


def to_peer(value):
    return send(value, lambda y, x, c, z: (y, x, 1 - c, z))


def along_x(d):
    return lambda y, x, c, z: (y, (x + d) % X, c, z)


def along_y(d):
    return lambda y, x, c, z: ((y + d) % Y, x, c, z)


def in_order(parts, me, axis):
    n = len(parts)
    ordered = []
    for j in range(n):
        pick = parts[0]
        for d in range(1, n):
            pick = jnp.where(lax.rem(me - j + n, n) == d, parts[d], pick)
        ordered.append(pick)
    return jnp.concatenate(ordered, axis=axis)


def times_t(vector_t, matrix):
    return lax.dot_general(
        vector_t, matrix.astype(jnp.float32), (((1,), (1,)), ((), ())),
        preferred_element_type=jnp.float32, precision=HIGHEST,
    )


def local(inverses, lower, forcing, inflow):
    group = lax.axis_index("group")
    z = lax.axis_index("blk")
    y, x, c = group // (X * CORES), (group // CORES) % X, group % CORES
    rows = inverses.shape[1]
    chip = rows * CORES
    block = chip * X

    def pick(array, k):
        return lax.dynamic_index_in_dim(array, k, 0, keepdims=False)

    def both(own, axis):
        def join(mine, theirs):
            return jnp.where(
                c == 0,
                jnp.concatenate([mine, theirs], axis=axis),
                jnp.concatenate([theirs, mine], axis=axis),
            )
        return join

    def station(array, axis):
        theirs = to_peer(pick(array, 1 - c))
        return both(None, axis)(pick(array, c), theirs)

    low = station(lower, 0)
    inv = station(inverses, 0)
    forcing_t = jnp.swapaxes(forcing, 1, 2).astype(jnp.float32)
    inflow_t = inflow.T
    small = jnp.stack([
        jnp.concatenate([forcing_t[0], inflow_t], axis=0),
        jnp.concatenate([forcing_t[1], inflow_t], axis=0),
    ])
    small = station(small, 1)

    def columns(xx):
        return lax.dynamic_slice_in_dim(low, lax.rem(xx, X) * block, block, 1)

    low_parts = [columns(x)] + [send(columns(x + d), along_x(d)) for d in range(1, X)]
    small_parts = [small] + [send(small, along_x(d)) for d in range(1, X)]
    inv_parts = [inv] + [send(inv, along_x(d)) for d in range(1, X)]
    low_block = in_order(low_parts, x, 0)
    small_block = in_order(small_parts, x, 1)
    low_panel = in_order([low_block] + [send(low_block, along_y(d)) for d in range(1, Y)], y, 0)
    small_all = in_order([small_block] + [send(small_block, along_y(d)) for d in range(1, Y)], y, 1)
    inv_panel = in_order(inv_parts, x, 0)

    forcing_all = small_all[:32].astype(jnp.bfloat16)
    entry_x = lax.dynamic_slice_in_dim(small_all[32:], x * block, block, 1)
    coupling = jnp.dot(inv_panel, low_panel, preferred_element_type=jnp.float32).astype(jnp.bfloat16)
    local_t = lax.dot_general(
        forcing_all, inv_panel, (((1,), (1,)), ((), ())), preferred_element_type=jnp.float32
    )
    local_t = jnp.where(x == 0, local_t, 0.0)
    entry_x = jnp.where(z == 0, entry_x, 0.0)
    share = local_t - jnp.where(c == 0, times_t(entry_x, coupling), 0.0)

    def across(d):
        def target(y, x, c, z):
            return ((y + d) % Y, x, c, z) if c == 0 else (y, (x + d) % X, c, z)
        return target

    turn = jnp.where(c == 0, y, x)
    panel = in_order([coupling] + [send(coupling, across(d)) for d in range(1, X)], turn, 0)
    shares = in_order([share] + [send(share, across(d)) for d in range(1, X)], turn, 1)
    panel_peer = to_peer(panel)
    shares_peer = to_peer(shares)
    share_peer = to_peer(share)
    first = jnp.where(c == 0, panel, panel_peer)
    second = jnp.where(c == 0, panel_peer, panel)
    first_shares = jnp.where(c == 0, shares, shares_peer)
    first_share = jnp.where(c == 0, share, share_peer)
    second_share = jnp.where(c == 0, share_peer, share)
    second = second.reshape(X, block, block).swapaxes(0, 1).reshape(block, X * block)

    product = jnp.dot(second, first, preferred_element_type=jnp.float32)
    base = second_share - times_t(first_shares, second)

    entry = jnp.zeros((32, block), jnp.float32)
    for _ in range(Z - 1):
        out = base + times_t(entry, product)
        arrived = [
            send(out, lambda y, x, c, z, d=d: ((x + d) % Y, y, c, z + 1) if z + 1 < Z else None)
            for d in range(X)
        ]
        entry = (arrived[0] + arrived[1]) + (arrived[2] + arrived[3])

    own_first = lax.dynamic_slice_in_dim(first, y * block, block, 0)
    finals = jnp.stack([
        first_share - times_t(entry, own_first),
        base + times_t(entry, product),
    ])
    finals = jnp.swapaxes(finals, 1, 2)

    def piece(xx):
        return lax.dynamic_slice_in_dim(finals, lax.rem(xx, X) * chip + c * rows, rows, 1)

    total = piece(x)
    for d in range(1, X):
        total = total + send(piece(x + d), along_x(d))
    return total


def solution(mesh):
    placed = (
        P("blk", "group", None),
        P("blk", "group", None),
        P("blk", "group", None),
        P("group", None),
    )
    return jax.shard_map(
        local, mesh=mesh, in_specs=placed, out_specs=P("blk", "group", None), check_vma=False
    )
```

```python
import jax
import jax.numpy as jnp
from jax import lax
from jax.experimental import pallas as pl
from jax.experimental.pallas import tpu as pltpu
from jax.sharding import PartitionSpec as P

Y, X, CORES, Z = 4, 4, 2, 4
AXES = ("group", "blk")
ROWS = 48
CHIP = ROWS * CORES
BLOCK = CHIP * X
N = BLOCK * Y
R = 32
F32, BF16 = jnp.float32, jnp.bfloat16


def send(value, target):
    pairs = []
    for y in range(Y):
        for x in range(X):
            for c in range(CORES):
                for z in range(Z):
                    to = target(y, x, c, z)
                    if to is not None:
                        ty, tx, tc, tz = to
                        pairs.append((
                            ((y * X + x) * CORES + c) * Z + z,
                            ((ty % Y * X + tx % X) * CORES + tc) * Z + tz,
                        ))
    return lax.ppermute(value, AXES, pairs)


def to_peer(value):
    return send(value, lambda y, x, c, z: (y, x, 1 - c, z))


def along_x(d):
    return lambda y, x, c, z: (y, x + d, c, z)


def along_y(d):
    return lambda y, x, c, z: (y + d, x, c, z)


def across(d):
    return lambda y, x, c, z: (y + d, x, c, z) if c == 0 else (y, x + d, c, z)


def place():
    group = lax.axis_index("group")
    return group // (X * CORES), (group // CORES) % X, group % CORES, lax.axis_index("blk")


def call(kernel, out, *args, scratch=(), flops=0):
    moved = sum(a.size * a.dtype.itemsize for a in args)
    return pl.pallas_call(
        kernel,
        out_shape=out,
        in_specs=[pl.BlockSpec(memory_space=pltpu.VMEM)] * len(args),
        out_specs=jax.tree.map(lambda _: pl.BlockSpec(memory_space=pltpu.VMEM), out),
        scratch_shapes=list(scratch),
        cost_estimate=pl.CostEstimate(flops=flops, bytes_accessed=moved, transcendentals=0),
        compiler_params=pltpu.CompilerParams(vmem_limit_bytes=24 * 2**20),
    )(*args)


def shape(dims, kind=BF16):
    return jax.ShapeDtypeStruct(dims, kind)


def nt(a, b):
    return lax.dot_general(a, b, (((1,), (1,)), ((), ())), preferred_element_type=F32)


def halves(value):
    high = value.astype(BF16)
    return high, (value - high.astype(F32)).astype(BF16)


def wide_nt(value, matrix):
    high, low = halves(value)
    return nt(high, matrix) + nt(low, matrix)


def lower_pieces(own, peer, *outs):
    y, x, c, _ = place()
    for d in range(X):
        columns = pl.ds(pl.multiple_of(lax.rem(x + d, X) * BLOCK, 128), BLOCK)
        outs[d][pl.ds(pl.multiple_of(c * ROWS, 16), ROWS), :] = own[c, :, columns]
        outs[d][pl.ds(pl.multiple_of((1 - c) * ROWS, 16), ROWS), :] = peer[c, :, columns]


def inverse_piece(own, peer, out):
    c = place()[2]
    out[pl.ds(pl.multiple_of(c * ROWS, 16), ROWS), :] = own[c]
    out[pl.ds(pl.multiple_of((1 - c) * ROWS, 16), ROWS), :] = peer[c]


def lower_block(p0, p1, p2, p3, forcing, out):
    x = place()[1]
    for d, piece in enumerate((p0, p1, p2, p3)):
        at = lax.rem(x - d + X, X) * CHIP
        out[pl.ds(pl.multiple_of(at, 16), CHIP), :] = piece[...]
    out[BLOCK:, :] = forcing[...]


def coupling_block(a0, a1, a2, a3, l0, l1, l2, l3, r0, r1, s0, s1, out, panel):
    y, x, c, z = place()
    for d, piece in enumerate((a0, a1, a2, a3)):
        at = lax.rem(x - d + X, X) * CHIP
        panel[pl.ds(pl.multiple_of(at, 16), CHIP), :] = piece[...]
    total = jnp.zeros((BLOCK, BLOCK), F32)
    share = jnp.zeros((R, BLOCK), F32)
    for d, piece in enumerate((l0, l1, l2, l3)):
        at = pl.multiple_of(lax.rem(y - d + Y, Y) * BLOCK, 128)
        part = panel[:, pl.ds(at, BLOCK)]
        total += jnp.dot(part, piece[:BLOCK, :], preferred_element_type=F32)
        share += nt(piece[BLOCK:, :], part)
    block = total.astype(BF16)
    entry = (r0[...] + r1[...]) + (s0[...] + s1[...])
    entry = jnp.where((z == 0) & (c == 0), entry, 0.0)
    share = share - wide_nt(entry, block)
    high, low = halves(share)
    out[:BLOCK, :] = block
    out[BLOCK:BLOCK + R, :] = high
    out[BLOCK + R:, :] = low


def product_block(o0, o1, o2, o3, p0, p1, p2, p3, high_out, low_out, base_out, second):
    y, x, c, _ = place()

    def run(firsts, seconds):
        for d, piece in enumerate(seconds):
            second[lax.rem(x - d + X, X)] = piece[:BLOCK, :]
        total = jnp.zeros((BLOCK, BLOCK), F32)
        base = seconds[0][BLOCK:BLOCK + R, :].astype(F32) + seconds[0][BLOCK + R:, :].astype(F32)
        for d, piece in enumerate(firsts):
            mine = second[lax.rem(y - d + Y, Y)]
            total += jnp.dot(mine, piece[:BLOCK, :], preferred_element_type=F32)
            both = nt(piece[BLOCK:, :], mine)
            base -= both[:R] + both[R:]
        high, low = halves(total)
        high_out[...] = high
        low_out[...] = low
        base_out[...] = base

    own, peer = (o0, o1, o2, o3), (p0, p1, p2, p3)

    @pl.when(c == 0)
    def _():
        run(own, peer)

    @pl.when(c != 0)
    def _():
        run(peer, own)


def gathered(r0, r1, s0, s1):
    return (r0[...] + r1[...]) + (s0[...] + s1[...])


def hop_block(r0, r1, s0, s1, p_high, p_low, base, out):
    entry = gathered(r0, r1, s0, s1)
    high, low = halves(entry)
    out[...] = base[...] + (nt(high, p_high[...]) + (nt(low, p_high[...]) + nt(high, p_low[...])))


def final_block(r0, r1, s0, s1, p_high, p_low, base, own, peer, *outs):
    y, x, c, _ = place()
    scratch = outs[-1]
    outs = outs[:-1]
    entry = gathered(r0, r1, s0, s1)
    high, low = halves(entry)
    second = base[...] + (nt(high, p_high[...]) + (nt(low, p_high[...]) + nt(high, p_low[...])))
    first_block = jnp.where(c == 0, own[...], peer[...])
    first = first_block[BLOCK:BLOCK + R, :].astype(F32) + first_block[BLOCK + R:, :].astype(F32)
    first = first - (nt(high, first_block[:BLOCK, :]) + nt(low, first_block[:BLOCK, :]))
    scratch[0] = first.T
    scratch[1] = second.T
    for d in range(X):
        at = lax.rem(x + d, X) * CHIP + c * ROWS
        outs[d][...] = scratch[:, pl.ds(pl.multiple_of(at, 16), ROWS), :]


def hop(out, shift):
    arrived = []
    for j in range(2):
        def target(y, x, c, z, j=j):
            if shift == 0:
                return (x + 2 * j + c, y, c, z) if z == 0 else None
            return (x + 2 * j + c, y, c, z + 1) if z + 1 < Z else None
        arrived.append(send(out, target))
    return arrived + [to_peer(value) for value in arrived]


def local(inverses, lower, forcing, inflow):
    y, x, c, z = place()

    forcing_t = jnp.swapaxes(forcing, 1, 2).astype(F32).reshape(2 * R, ROWS)
    small = jnp.concatenate([forcing_t, inflow.T], axis=0)
    lower_peer = to_peer(lower)
    small_peer = to_peer(small)
    inverses_peer = to_peer(inverses)
    small = jnp.where(
        c == 0,
        jnp.concatenate([small, small_peer], axis=1),
        jnp.concatenate([small_peer, small], axis=1),
    )
    at_x = jnp.zeros((3 * R, BLOCK), F32)
    at_x = lax.dynamic_update_slice(at_x, small, (0, x * CHIP))
    forcing_x = lax.dynamic_slice_in_dim(at_x, c * R, R, 0).astype(BF16)
    inflow_x = at_x[2 * R:]

    piece = shape((CHIP, BLOCK))
    low = call(lower_pieces, [piece] * X, lower, lower_peer)
    low = [low[0]] + [send(low[d], along_x(d)) for d in range(1, X)]
    own = call(lower_block, shape((BLOCK + R, BLOCK)), *low, forcing_x)
    inverses, inverses_peer, own = lax.optimization_barrier((inverses, inverses_peer, own))
    panel = [own] + [send(own, along_y(d)) for d in range(1, Y)]
    inv = call(inverse_piece, shape((CHIP, N)), inverses, inverses_peer)
    inv = [inv] + [send(inv, along_x(d)) for d in range(1, X)]
    entry = hop(inflow_x, 0)

    message = call(
        coupling_block, shape((BLOCK + 2 * R, BLOCK)), *inv, *panel, *entry,
        scratch=[pltpu.VMEM((BLOCK, N), BF16)], flops=2 * BLOCK * BLOCK * N,
    )
    turn = [message] + [send(message, across(d)) for d in range(1, X)]
    turn_peer = [to_peer(value) for value in turn]
    p_high, p_low, base = call(
        product_block, [shape((BLOCK, BLOCK)), shape((BLOCK, BLOCK)), shape((R, BLOCK), F32)],
        *turn, *turn_peer, scratch=[pltpu.VMEM((X, BLOCK, BLOCK), BF16)], flops=2 * BLOCK * BLOCK * N,
    )

    out = base
    for step in range(Z - 1):
        entry = hop(out, 1)
        if step + 1 < Z - 1:
            out = call(hop_block, shape((R, BLOCK), F32), *entry, p_high, p_low, base)
    part = shape((2, ROWS, R), F32)
    finals = call(
        final_block, [part] * X, *entry, p_high, p_low, base, turn[0], turn_peer[0],
        scratch=[pltpu.VMEM((2, BLOCK, R), F32)],
    )
    total = finals[0]
    for d in range(1, X):
        total = total + send(finals[d], along_x(d))
    return total


def solution(mesh):
    placed = (
        P("blk", "group", None),
        P("blk", "group", None),
        P("blk", "group", None),
        P("group", None),
    )
    return jax.shard_map(
        local, mesh=mesh, in_specs=placed, out_specs=P("blk", "group", None), check_vma=False
    )
```

```python
import jax
import jax.numpy as jnp
from jax import lax
from jax.experimental import pallas as pl
from jax.experimental.pallas import tpu as pltpu
from jax.sharding import PartitionSpec as P

Y, X, CORES, Z = 4, 4, 2, 4
AXES = ("group", "blk")
ROWS = 48
CHIP = ROWS * CORES
BLOCK = CHIP * X
N = BLOCK * Y
R = 32
LANES = 128
F32, BF16 = jnp.float32, jnp.bfloat16


def send(value, target):
    pairs = []
    for y in range(Y):
        for x in range(X):
            for c in range(CORES):
                for z in range(Z):
                    to = target(y, x, c, z)
                    if to is not None:
                        ty, tx, tc, tz = to
                        pairs.append((
                            ((y * X + x) * CORES + c) * Z + z,
                            ((ty % Y * X + tx % X) * CORES + tc) * Z + tz,
                        ))
    return lax.ppermute(value, AXES, pairs)


def to_peer(value):
    return send(value, lambda y, x, c, z: (y, x, 1 - c, z))


def along_v(d):
    return lambda y, x, c, z: (y, x + d, c, z) if z % 2 == 0 else (y + d, x, c, z)


def along_u(d):
    return lambda y, x, c, z: (y + d, x, c, z) if z % 2 == 0 else (y, x + d, c, z)


def across(d):
    return lambda y, x, c, z: (along_u(d) if c == 0 else along_v(d))(y, x, c, z)


def place():
    group, z = lax.axis_index("group"), lax.axis_index("blk")
    y, x = group // (X * CORES), (group // CORES) % X
    even = z % 2 == 0
    return jnp.where(even, y, x), jnp.where(even, x, y), group % CORES, z


def chunk(u, v, z):
    return pl.multiple_of(jnp.where(z % 2 == 0, u * BLOCK + v * CHIP, v * BLOCK + u * CHIP), 32)


def rows_at(start, size):
    return pl.ds(pl.multiple_of(start, 16), size)


def lanes_at(start, size):
    return pl.ds(pl.multiple_of(start, 128), size)


def behind(me, d):
    return lax.rem(me - d + 4, 4)


def call(kernel, out, *args, scratch=(), flops=0):
    moved = sum(a.size * a.dtype.itemsize for a in args)
    return pl.pallas_call(
        kernel,
        out_shape=out,
        in_specs=[pl.BlockSpec(memory_space=pltpu.VMEM)] * len(args),
        out_specs=jax.tree.map(lambda _: pl.BlockSpec(memory_space=pltpu.VMEM), out),
        scratch_shapes=list(scratch),
        cost_estimate=pl.CostEstimate(flops=flops, bytes_accessed=moved, transcendentals=0),
        compiler_params=pltpu.CompilerParams(vmem_limit_bytes=24 * 2**20),
    )(*args)


def shape(dims, kind=BF16):
    return jax.ShapeDtypeStruct(dims, kind)


def nt(a, b):
    return lax.dot_general(a, b, (((1,), (1,)), ((), ())), preferred_element_type=F32)


def halves(value):
    high = value.astype(BF16)
    return high, (value - high.astype(F32)).astype(BF16)


def lower_pieces(own, peer, *refs):
    outs, rows, cut = refs[:4], refs[4], refs[5]
    _, v, c, z = place()
    rows[rows_at(c * ROWS, ROWS), :] = own[c]
    rows[rows_at((1 - c) * ROWS, ROWS), :] = peer[c]

    @pl.when(z % 2 == 0)
    def _():
        for b in range(4):
            cut[b] = jnp.concatenate(
                [rows[:, i * BLOCK + b * CHIP:i * BLOCK + (b + 1) * CHIP] for i in range(4)], axis=1
            )

    @pl.when(z % 2 == 1)
    def _():
        for b in range(4):
            cut[b] = rows[:, b * BLOCK:(b + 1) * BLOCK]

    for d in range(4):
        outs[d][...] = cut[lax.rem(v + d, 4)]


def inverse_piece(own, peer, out):
    c = place()[2]
    out[rows_at(c * ROWS, ROWS), :] = own[c]
    out[rows_at((1 - c) * ROWS, ROWS), :] = peer[c]


def lower_block(p0, p1, p2, p3, forcing, forcing_peer, inflow, inflow_peer, out, sides):
    _, v, c, _ = place()
    for d, piece in enumerate((p0, p1, p2, p3)):
        out[rows_at(behind(v, d) * CHIP, CHIP), :] = piece[...]
    sides[...] = jnp.zeros_like(sides)
    for f, e, at in ((forcing, inflow, c * ROWS), (forcing_peer, inflow_peer, (1 - c) * ROWS)):
        high, low = halves(e[...])
        sides[rows_at(at, ROWS), 0:R] = f[c].astype(F32)
        sides[rows_at(at, ROWS), R:2 * R] = high.astype(F32)
        sides[rows_at(at, ROWS), 2 * R:3 * R] = low.astype(F32)
    for g in range(3):
        out[BLOCK:, g * LANES:(g + 1) * LANES] = sides[g * R:(g + 1) * R, :].astype(BF16)


def coupling_block(a0, a1, a2, a3, l0, l1, l2, l3, out, panel, lower, sides, entry):
    u, v, c, z = place()
    for d, piece in enumerate((a0, a1, a2, a3)):
        panel[rows_at(behind(v, d) * CHIP, CHIP), :] = piece[...]
    sides[...] = jnp.zeros_like(sides)
    for d, piece in enumerate((l0, l1, l2, l3)):
        from_u = behind(u, d)
        for j in range(4):
            lower[rows_at(chunk(from_u, j, z), CHIP), :] = piece[j * CHIP:(j + 1) * CHIP, :]
        at = chunk(from_u, v, z)
        for g in range(3):
            part = piece[BLOCK:, g * LANES:(g + 1) * LANES]
            sides[rows_at(at + g * R, R), :] = part
            entry[rows_at(from_u * CHIP + g * R, R), :] = part
    block = jnp.dot(panel[...], lower[...], preferred_element_type=F32).astype(BF16)
    share = jnp.dot(panel[...], sides[...], preferred_element_type=F32)[:, :R]
    known = jnp.dot(block, entry[...], preferred_element_type=F32)
    known = known[:, R:2 * R] + known[:, 2 * R:3 * R]
    share = share - jnp.where((z == 0) & (c == 0), known, 0.0)
    share = jnp.concatenate([share, jnp.zeros((BLOCK, LANES - R), F32)], axis=1).T[:R]
    high, low = halves(share)
    out[:BLOCK, :] = block
    out[BLOCK:BLOCK + R, :] = high
    out[BLOCK + R:, :] = low


def product_block(o0, o1, o2, o3, p0, p1, p2, p3, high_out, low_out, base_out, second, first, shares):
    u, v, c, _ = place()

    def run(firsts, seconds):
        for d, piece in enumerate(seconds):
            second[:, lanes_at(behind(v, d) * BLOCK, BLOCK)] = piece[:BLOCK, :]
        for d, piece in enumerate(firsts):
            from_u = behind(u, d)
            side = piece[BLOCK:, :].astype(F32)
            side = jnp.concatenate([side, jnp.zeros((LANES - 2 * R, BLOCK), F32)], axis=0).T.astype(BF16)
            for j in range(4):
                at = rows_at(j * BLOCK + from_u * CHIP, CHIP)
                first[at, :] = piece[j * CHIP:(j + 1) * CHIP, :]
                shares[at, :] = side[j * CHIP:(j + 1) * CHIP, :]
        total = jnp.dot(second[...], first[...], preferred_element_type=F32)
        taken = jnp.dot(second[...], shares[...], preferred_element_type=F32).T
        high, low = halves(total)
        high_out[...] = high
        low_out[...] = low
        own = seconds[0][BLOCK:BLOCK + R, :].astype(F32) + seconds[0][BLOCK + R:, :].astype(F32)
        base_out[...] = own - (taken[:R] + taken[R:2 * R])

    own, peer = (o0, o1, o2, o3), (p0, p1, p2, p3)

    @pl.when(c == 0)
    def _():
        run(own, peer)

    @pl.when(c != 0)
    def _():
        run(peer, own)


def gathered(r0, r1, s0, s1):
    return (r0[...] + r1[...]) + (s0[...] + s1[...])


def hop_block(r0, r1, s0, s1, p_high, p_low, base, out):
    entry = gathered(r0, r1, s0, s1)
    high, low = halves(entry)
    out[...] = base[...] + (nt(high, p_high[...]) + (nt(low, p_high[...]) + nt(high, p_low[...])))


def final_block(r0, r1, s0, s1, p_high, p_low, base, own, peer, *outs):
    c = place()[2]
    v = place()[1]
    scratch = outs[-1]
    outs = outs[:-1]
    entry = gathered(r0, r1, s0, s1)
    high, low = halves(entry)
    second = base[...] + (nt(high, p_high[...]) + (nt(low, p_high[...]) + nt(high, p_low[...])))
    first_block = jnp.where(c == 0, own[...], peer[...])
    first = first_block[BLOCK:BLOCK + R, :].astype(F32) + first_block[BLOCK + R:, :].astype(F32)
    first = first - (nt(high, first_block[:BLOCK, :]) + nt(low, first_block[:BLOCK, :]))
    scratch[0] = first.T
    scratch[1] = second.T
    for d in range(X):
        outs[d][...] = scratch[:, rows_at(lax.rem(v + d, 4) * CHIP + c * ROWS, ROWS), :]


def hop(out):
    arrived = []
    for j in range(2):
        def target(y, x, c, z, j=j):
            y, x, c, _ = along_v(2 * j + c)(y, x, c, z)
            return (y, x, c, z + 1) if z + 1 < Z else None
        arrived.append(send(out, target))
    return arrived + [to_peer(value) for value in arrived]


def local(inverses, lower, forcing, inflow):
    lower_peer = to_peer(lower)
    piece = shape((CHIP, BLOCK))
    low = call(
        lower_pieces, [piece] * 4, lower, lower_peer,
        scratch=[pltpu.VMEM((CHIP, N), BF16), pltpu.VMEM((4, CHIP, BLOCK), BF16)],
    )
    low = [low[0]] + [send(low[d], along_v(d)) for d in range(1, 4)]
    forcing_peer = to_peer(forcing)
    inflow_peer = to_peer(inflow)
    own = call(
        lower_block, shape((BLOCK + R, BLOCK)), *low, forcing, forcing_peer, inflow, inflow_peer,
        scratch=[pltpu.VMEM((CHIP, LANES), F32)],
    )
    inverses, own = lax.optimization_barrier((inverses, own))
    panel = [own] + [send(own, along_u(d)) for d in range(1, 4)]
    inverses_peer = to_peer(inverses)
    inv = call(inverse_piece, shape((CHIP, N)), inverses, inverses_peer)
    inv = [inv] + [send(inv, along_v(d)) for d in range(1, 4)]

    message = call(
        coupling_block, shape((BLOCK + 2 * R, BLOCK)), *inv, *panel,
        scratch=[
            pltpu.VMEM((BLOCK, N), BF16), pltpu.VMEM((N, BLOCK), BF16),
            pltpu.VMEM((N, LANES), BF16), pltpu.VMEM((BLOCK, LANES), BF16),
        ],
        flops=2 * BLOCK * BLOCK * N,
    )
    turn = [message] + [send(message, across(d)) for d in range(1, 4)]
    turn_peer = [to_peer(value) for value in turn]
    p_high, p_low, base = call(
        product_block, [shape((BLOCK, BLOCK)), shape((BLOCK, BLOCK)), shape((R, BLOCK), F32)],
        *turn, *turn_peer,
        scratch=[pltpu.VMEM((BLOCK, N), BF16), pltpu.VMEM((N, BLOCK), BF16), pltpu.VMEM((N, LANES), BF16)],
        flops=2 * BLOCK * BLOCK * N,
    )

    out = base
    for step in range(Z - 1):
        entry = hop(out)
        if step + 1 < Z - 1:
            out = call(hop_block, shape((R, BLOCK), F32), *entry, p_high, p_low, base)
    part = shape((2, ROWS, R), F32)
    finals = call(
        final_block, [part] * 4, *entry, p_high, p_low, base, turn[0], turn_peer[0],
        scratch=[pltpu.VMEM((2, BLOCK, R), F32)],
    )
    total = finals[0]
    for d in range(1, 4):
        total = total + send(finals[d], along_v(d))
    return total


def solution(mesh):
    placed = (
        P("blk", "group", None),
        P("blk", "group", None),
        P("blk", "group", None),
        P("group", None),
    )
    return jax.shard_map(
        local, mesh=mesh, in_specs=placed, out_specs=P("blk", "group", None), check_vma=False
    )
```

```python
import jax
import jax.numpy as jnp
from jax import lax
from jax.experimental import pallas as pl
from jax.experimental.pallas import tpu as pltpu
from jax.sharding import PartitionSpec as P

Y, X, CORES, Z = 4, 4, 2, 4
AXES = ("group", "blk")
ROWS = 48
CHIP = ROWS * CORES
BLOCK = CHIP * X
N = BLOCK * Y
R = 32
LANES = 128
F32, BF16 = jnp.float32, jnp.bfloat16


def send(value, target):
    pairs = []
    for y in range(Y):
        for x in range(X):
            for c in range(CORES):
                for z in range(Z):
                    to = target(y, x, c, z)
                    if to is not None:
                        ty, tx, tc, tz = to
                        pairs.append((
                            ((y * X + x) * CORES + c) * Z + z,
                            ((ty % Y * X + tx % X) * CORES + tc) * Z + tz,
                        ))
    return lax.ppermute(value, AXES, pairs)


def to_peer(value):
    return send(value, lambda y, x, c, z: (y, x, 1 - c, z))


def along_v(d):
    return lambda y, x, c, z: (y, x + d, c, z) if z % 2 == 0 else (y + d, x, c, z)


def along_u(d):
    return lambda y, x, c, z: (y + d, x, c, z) if z % 2 == 0 else (y, x + d, c, z)


def across(d):
    return lambda y, x, c, z: (along_u(d) if c == 0 else along_v(d))(y, x, c, z)


def place():
    group, z = lax.axis_index("group"), lax.axis_index("blk")
    y, x = group // (X * CORES), (group // CORES) % X
    even = z % 2 == 0
    return jnp.where(even, y, x), jnp.where(even, x, y), group % CORES, z


def chunk(u, v, z):
    return pl.multiple_of(jnp.where(z % 2 == 0, u * BLOCK + v * CHIP, v * BLOCK + u * CHIP), 32)


def rows_at(start, size):
    return pl.ds(pl.multiple_of(start, 16), size)


def lanes_at(start, size):
    return pl.ds(pl.multiple_of(start, 128), size)


def behind(me, d):
    return lax.rem(me - d + 4, 4)


def call(kernel, out, *args, scratch=(), flops=0):
    moved = sum(a.size * a.dtype.itemsize for a in args)
    return pl.pallas_call(
        kernel,
        out_shape=out,
        in_specs=[pl.BlockSpec(memory_space=pltpu.VMEM)] * len(args),
        out_specs=jax.tree.map(lambda _: pl.BlockSpec(memory_space=pltpu.VMEM), out),
        scratch_shapes=list(scratch),
        cost_estimate=pl.CostEstimate(flops=flops, bytes_accessed=moved, transcendentals=0),
        compiler_params=pltpu.CompilerParams(vmem_limit_bytes=24 * 2**20),
    )(*args)


def shape(dims, kind=BF16):
    return jax.ShapeDtypeStruct(dims, kind)


def nt(a, b):
    return lax.dot_general(a, b, (((1,), (1,)), ((), ())), preferred_element_type=F32)


def halves(value):
    high = value.astype(BF16)
    return high, (value - high.astype(F32)).astype(BF16)


def hold(own, out):
    out[...] = own[place()[2]]


def lower_pieces(own, peer, *refs):
    outs, rows, cut = refs[:4], refs[4], refs[5]
    _, v, c, z = place()
    rows[rows_at(c * ROWS, ROWS), :] = own[...]
    rows[rows_at((1 - c) * ROWS, ROWS), :] = peer[c]

    @pl.when(z % 2 == 0)
    def _():
        for b in range(4):
            cut[b] = jnp.concatenate(
                [rows[:, i * BLOCK + b * CHIP:i * BLOCK + (b + 1) * CHIP] for i in range(4)], axis=1
            )

    @pl.when(z % 2 == 1)
    def _():
        for b in range(4):
            cut[b] = rows[:, b * BLOCK:(b + 1) * BLOCK]

    for d in range(4):
        outs[d][...] = cut[lax.rem(v + d, 4)]


def inverse_piece(own, peer, out):
    c = place()[2]
    out[rows_at(c * ROWS, ROWS), :] = own[c]
    out[rows_at((1 - c) * ROWS, ROWS), :] = peer[c]


def lower_block(p0, p1, p2, p3, forcing, forcing_peer, inflow, inflow_peer, out, sides):
    _, v, c, _ = place()
    for d, piece in enumerate((p0, p1, p2, p3)):
        out[rows_at(behind(v, d) * CHIP, CHIP), :] = piece[...]
    for f, e, at in ((forcing, inflow, c * ROWS), (forcing_peer, inflow_peer, (1 - c) * ROWS)):
        high, low = halves(e[...])
        side = jnp.concatenate([f[c].astype(F32), high.astype(F32), low.astype(F32), jnp.zeros((R, ROWS), F32)], axis=0)
        side = jnp.concatenate([side, jnp.zeros((LANES, LANES - ROWS), F32)], axis=1).T
        sides[rows_at(at, ROWS), :] = side[:ROWS]
    for g in range(3):
        out[BLOCK:, g * LANES:(g + 1) * LANES] = sides[g * R:(g + 1) * R, :].astype(BF16)


def coupling_block(a0, a1, a2, a3, l0, l1, l2, l3, out, panel, lower, sides, entry):
    u, v, c, z = place()
    for d, piece in enumerate((a0, a1, a2, a3)):
        panel[rows_at(behind(v, d) * CHIP, CHIP), :] = piece[...]
    sides[...] = jnp.zeros_like(sides)
    for d, piece in enumerate((l0, l1, l2, l3)):
        from_u = behind(u, d)
        for j in range(4):
            lower[rows_at(chunk(from_u, j, z), CHIP), :] = piece[j * CHIP:(j + 1) * CHIP, :]
        at = chunk(from_u, v, z)
        for g in range(3):
            part = piece[BLOCK:, g * LANES:(g + 1) * LANES]
            sides[rows_at(at + g * R, R), :] = part
            entry[rows_at(from_u * CHIP + g * R, R), :] = part
    block = jnp.dot(panel[...], lower[...], preferred_element_type=F32).astype(BF16)
    share = jnp.dot(panel[...], sides[...], preferred_element_type=F32)[:, :R]
    known = jnp.dot(block, entry[...], preferred_element_type=F32)
    known = known[:, R:2 * R] + known[:, 2 * R:3 * R]
    share = share - jnp.where((z == 0) & (c == 0), known, 0.0)
    share = jnp.concatenate([share, jnp.zeros((BLOCK, LANES - R), F32)], axis=1).T[:R]
    high, low = halves(share)
    out[:BLOCK, :] = block
    out[BLOCK:BLOCK + R, :] = high
    out[BLOCK + R:, :] = low


def product_block(o0, o1, o2, o3, p0, p1, p2, p3, high_out, low_out, base_out, start_out, second, first, shares):
    u, v, c, _ = place()

    def run(firsts, seconds):
        for d, piece in enumerate(seconds):
            second[:, lanes_at(behind(v, d) * BLOCK, BLOCK)] = piece[:BLOCK, :]
        for d, piece in enumerate(firsts):
            from_u = behind(u, d)
            side = piece[BLOCK:, :].astype(F32)
            side = jnp.concatenate([side, jnp.zeros((LANES - 2 * R, BLOCK), F32)], axis=0).T.astype(BF16)
            for j in range(4):
                at = rows_at(j * BLOCK + from_u * CHIP, CHIP)
                first[at, :] = piece[j * CHIP:(j + 1) * CHIP, :]
                shares[at, :] = side[j * CHIP:(j + 1) * CHIP, :]
        total = jnp.dot(second[...], first[...], preferred_element_type=F32)
        taken = jnp.dot(second[...], shares[...], preferred_element_type=F32).T
        high, low = halves(total)
        high_out[...] = high
        low_out[...] = low
        own = seconds[0][BLOCK:BLOCK + R, :].astype(F32) + seconds[0][BLOCK + R:, :].astype(F32)
        base = own - (taken[:R] + taken[R:2 * R])
        base_out[...] = base
        start_out[...] = base.astype(BF16)

    own, peer = (o0, o1, o2, o3), (p0, p1, p2, p3)

    @pl.when(c == 0)
    def _():
        run(own, peer)

    @pl.when(c != 0)
    def _():
        run(peer, own)


def pair_sum(r0, r1, out):
    out[...] = r0[...].astype(F32) + r1[...].astype(F32)


def onward(entry, p_high, p_low, base):
    high, low = halves(entry)
    return base + (nt(high, p_high) + (nt(low, p_high) + nt(high, p_low)))


def hop_block(own, peer, p_high, p_low, base, out):
    out[...] = onward(own[...] + peer[...], p_high[...], p_low[...], base[...]).astype(BF16)


def final_block(own, peer, p_high, p_low, base, message, message_peer, *outs):
    _, v, c, _ = place()
    entry = own[...] + peer[...]
    high, low = halves(entry)
    second = onward(entry, p_high[...], p_low[...], base[...])
    first_block = jnp.where(c == 0, message[...], message_peer[...])
    first = first_block[BLOCK:BLOCK + R, :].astype(F32) + first_block[BLOCK + R:, :].astype(F32)
    first = first - (nt(high, first_block[:BLOCK, :]) + nt(low, first_block[:BLOCK, :]))
    states = jnp.concatenate([first, second], axis=0)
    for d in range(4):
        at = lax.rem(v + d, 4) * CHIP + c * ROWS
        outs[d][...] = pltpu.roll(states, lax.rem(BLOCK - at, BLOCK), 1)[:, :ROWS]


def hop(out):
    arrived = []
    for j in range(2):
        def target(y, x, c, z, j=j):
            y, x, c, _ = along_v(2 * j + c)(y, x, c, z)
            return (y, x, c, z + 1) if z + 1 < Z else None
        arrived.append(send(out, target))
    own = call(pair_sum, shape((R, BLOCK), F32), *arrived)
    return own, to_peer(own)


def local(inverses, lower, forcing, inflow):
    forcing = jnp.swapaxes(forcing, 1, 2)
    inflow = inflow.T
    inverses_peer = to_peer(inverses)
    lower_peer = to_peer(lower)
    inv_own = call(inverse_piece, shape((CHIP, N)), inverses, inverses_peer)
    lower_own = call(hold, shape((ROWS, N)), lower)
    inv_own, lower_own = lax.optimization_barrier((inv_own, lower_own))
    piece = shape((CHIP, BLOCK))
    low = call(
        lower_pieces, [piece] * 4, lower_own, lower_peer,
        scratch=[pltpu.VMEM((CHIP, N), BF16), pltpu.VMEM((4, CHIP, BLOCK), BF16)],
    )
    inv = {0: inv_own, 1: send(inv_own, along_v(1)), 3: send(inv_own, along_v(3))}
    low = [low[0]] + [send(low[d], along_v(d)) for d in range(1, 4)]
    forcing_peer = to_peer(forcing)
    inflow_peer = to_peer(inflow)
    inv, low = lax.optimization_barrier((inv, low))
    inv[2] = send(inv[0], along_v(2))
    inv = [inv[d] for d in range(4)]
    own = call(
        lower_block, shape((BLOCK + R, BLOCK)), *low, forcing, forcing_peer, inflow, inflow_peer,
        scratch=[pltpu.VMEM((CHIP, LANES), F32)],
    )
    panel = [own] + [send(own, along_u(d)) for d in range(1, 4)]

    message = call(
        coupling_block, shape((BLOCK + 2 * R, BLOCK)), *inv, *panel,
        scratch=[
            pltpu.VMEM((BLOCK, N), BF16), pltpu.VMEM((N, BLOCK), BF16),
            pltpu.VMEM((N, LANES), BF16), pltpu.VMEM((BLOCK, LANES), BF16),
        ],
        flops=2 * BLOCK * BLOCK * N,
    )
    turn = [message] + [send(message, across(d)) for d in range(1, 4)]
    turn_peer = [to_peer(value) for value in turn]
    p_high, p_low, base, out = call(
        product_block,
        [shape((BLOCK, BLOCK)), shape((BLOCK, BLOCK)), shape((R, BLOCK), F32), shape((R, BLOCK))],
        *turn, *turn_peer,
        scratch=[pltpu.VMEM((BLOCK, N), BF16), pltpu.VMEM((N, BLOCK), BF16), pltpu.VMEM((N, LANES), BF16)],
        flops=2 * BLOCK * BLOCK * N,
    )

    for step in range(Z - 1):
        entry = hop(out)
        if step + 1 < Z - 1:
            out = call(hop_block, shape((R, BLOCK)), *entry, p_high, p_low, base)
    finals = call(
        final_block, [shape((2 * R, ROWS), F32)] * 4, *entry, p_high, p_low, base, turn[0], turn_peer[0]
    )
    total = finals[0]
    for d in range(1, 4):
        total = total + send(finals[d], along_v(d))
    return jnp.swapaxes(total.reshape(2, R, ROWS), 1, 2)


def solution(mesh):
    placed = (
        P("blk", "group", None),
        P("blk", "group", None),
        P("blk", "group", None),
        P("group", None),
    )
    return jax.shard_map(
        local, mesh=mesh, in_specs=placed, out_specs=P("blk", "group", None), check_vma=False
    )
```

```python
import jax
import jax.numpy as jnp
from jax import lax
from jax.experimental import pallas as pl
from jax.experimental.pallas import tpu as pltpu
from jax.sharding import PartitionSpec as P

Y, X, CORES, Z = 4, 4, 2, 4
AXES = ("group", "blk")
ROWS = 48
CHIP = ROWS * CORES
BLOCK = CHIP * X
N = BLOCK * Y
R = 32
LANES = 128
F32, BF16 = jnp.float32, jnp.bfloat16


def send(value, target):
    pairs = []
    for y in range(Y):
        for x in range(X):
            for c in range(CORES):
                for z in range(Z):
                    to = target(y, x, c, z)
                    if to is not None:
                        ty, tx, tc, tz = to
                        pairs.append((
                            ((y * X + x) * CORES + c) * Z + z,
                            ((ty % Y * X + tx % X) * CORES + tc) * Z + tz,
                        ))
    return lax.ppermute(value, AXES, pairs)


def to_peer(value):
    return send(value, lambda y, x, c, z: (y, x, 1 - c, z))


def along_v(d):
    return lambda y, x, c, z: (y, x + d, c, z) if z % 2 == 0 else (y + d, x, c, z)


def along_u(d):
    return lambda y, x, c, z: (y + d, x, c, z) if z % 2 == 0 else (y, x + d, c, z)


def across(d):
    return lambda y, x, c, z: (along_u(d) if c == 0 else along_v(d))(y, x, c, z)


def place():
    group, z = lax.axis_index("group"), lax.axis_index("blk")
    y, x = group // (X * CORES), (group // CORES) % X
    even = z % 2 == 0
    return jnp.where(even, y, x), jnp.where(even, x, y), group % CORES, z


def chunk(u, v, z):
    return pl.multiple_of(jnp.where(z % 2 == 0, u * BLOCK + v * CHIP, v * BLOCK + u * CHIP), 32)


def rows_at(start, size):
    return pl.ds(pl.multiple_of(start, 16), size)


def lanes_at(start, size):
    return pl.ds(pl.multiple_of(start, 128), size)


def behind(me, d):
    return lax.rem(me - d + 4, 4)


def call(kernel, out, *args, scratch=(), flops=0):
    moved = sum(a.size * a.dtype.itemsize for a in args)
    return pl.pallas_call(
        kernel,
        out_shape=out,
        in_specs=[pl.BlockSpec(memory_space=pltpu.VMEM)] * len(args),
        out_specs=jax.tree.map(lambda _: pl.BlockSpec(memory_space=pltpu.VMEM), out),
        scratch_shapes=list(scratch),
        cost_estimate=pl.CostEstimate(flops=flops, bytes_accessed=moved, transcendentals=0),
        compiler_params=pltpu.CompilerParams(vmem_limit_bytes=24 * 2**20),
    )(*args)


def shape(dims, kind=BF16):
    return jax.ShapeDtypeStruct(dims, kind)


def nt(a, b):
    return lax.dot_general(a, b, (((1,), (1,)), ((), ())), preferred_element_type=F32)


def halves(value):
    high = value.astype(BF16)
    return high, (value - high.astype(F32)).astype(BF16)


def hold(own, out):
    out[...] = own[place()[2]]


def lower_pieces(own, peer, *refs):
    outs, rows, cut = refs[:4], refs[4], refs[5]
    _, v, c, z = place()
    rows[rows_at(c * ROWS, ROWS), :] = own[...]
    rows[rows_at((1 - c) * ROWS, ROWS), :] = peer[c]

    @pl.when(z % 2 == 0)
    def _():
        for b in range(4):
            cut[b] = jnp.concatenate(
                [rows[:, i * BLOCK + b * CHIP:i * BLOCK + (b + 1) * CHIP] for i in range(4)], axis=1
            )

    @pl.when(z % 2 == 1)
    def _():
        for b in range(4):
            cut[b] = rows[:, b * BLOCK:(b + 1) * BLOCK]

    for d in range(4):
        outs[d][...] = cut[lax.rem(v + d, 4)]


def inverse_piece(own, peer, out):
    c = place()[2]
    out[rows_at(c * ROWS, ROWS), :] = own[c]
    out[rows_at((1 - c) * ROWS, ROWS), :] = peer[c]


def inverse_panel(a0, a1, a2, a3, out):
    v = place()[1]
    for d, piece in enumerate((a0, a1, a2, a3)):
        out[rows_at(behind(v, d) * CHIP, CHIP), :] = piece[...]


def lower_block(p0, p1, p2, p3, forcing, forcing_peer, inflow, inflow_peer, out, sides):
    _, v, c, _ = place()
    for d, piece in enumerate((p0, p1, p2, p3)):
        out[rows_at(behind(v, d) * CHIP, CHIP), :] = piece[...]
    for f, e, at in ((forcing, inflow, c * ROWS), (forcing_peer, inflow_peer, (1 - c) * ROWS)):
        high, low = halves(e[...])
        side = jnp.concatenate([f[c].astype(F32), high.astype(F32), low.astype(F32), jnp.zeros((R, ROWS), F32)], axis=0)
        side = jnp.concatenate([side, jnp.zeros((LANES, LANES - ROWS), F32)], axis=1).T
        sides[rows_at(at, ROWS), :] = side[:ROWS]
    for g in range(3):
        out[BLOCK:, g * LANES:(g + 1) * LANES] = sides[g * R:(g + 1) * R, :].astype(BF16)


def coupling_block(panel, l0, l1, l2, l3, out, lower, sides, entry):
    u, v, c, z = place()
    sides[...] = jnp.zeros_like(sides)
    for d, piece in enumerate((l0, l1, l2, l3)):
        from_u = behind(u, d)
        for j in range(4):
            lower[rows_at(chunk(from_u, j, z), CHIP), :] = piece[j * CHIP:(j + 1) * CHIP, :]
        at = chunk(from_u, v, z)
        for g in range(3):
            part = piece[BLOCK:, g * LANES:(g + 1) * LANES]
            sides[rows_at(at + g * R, R), :] = part
            entry[rows_at(from_u * CHIP + g * R, R), :] = part
    block = jnp.dot(panel[...], lower[...], preferred_element_type=F32).astype(BF16)
    share = jnp.dot(panel[...], sides[...], preferred_element_type=F32)[:, :R]
    known = jnp.dot(block, entry[...], preferred_element_type=F32)
    known = known[:, R:2 * R] + known[:, 2 * R:3 * R]
    share = share - jnp.where((z == 0) & (c == 0), known, 0.0)
    share = jnp.concatenate([share, jnp.zeros((BLOCK, LANES - R), F32)], axis=1).T[:R]
    high, low = halves(share)
    out[:BLOCK, :] = block
    out[BLOCK:BLOCK + R, :] = high
    out[BLOCK + R:, :] = low


def product_block(o0, o1, o2, o3, p0, p1, p2, p3, high_out, low_out, base_out, start_out, second, first, shares):
    u, v, c, _ = place()

    def run(firsts, seconds):
        for d, piece in enumerate(seconds):
            second[:, lanes_at(behind(v, d) * BLOCK, BLOCK)] = piece[:BLOCK, :]
        for d, piece in enumerate(firsts):
            from_u = behind(u, d)
            side = piece[BLOCK:, :].astype(F32)
            side = jnp.concatenate([side, jnp.zeros((LANES - 2 * R, BLOCK), F32)], axis=0).T.astype(BF16)
            for j in range(4):
                at = rows_at(j * BLOCK + from_u * CHIP, CHIP)
                first[at, :] = piece[j * CHIP:(j + 1) * CHIP, :]
                shares[at, :] = side[j * CHIP:(j + 1) * CHIP, :]
        total = jnp.dot(second[...], first[...], preferred_element_type=F32)
        taken = jnp.dot(second[...], shares[...], preferred_element_type=F32).T
        high, low = halves(total)
        high_out[...] = high
        low_out[...] = low
        own = seconds[0][BLOCK:BLOCK + R, :].astype(F32) + seconds[0][BLOCK + R:, :].astype(F32)
        base = own - (taken[:R] + taken[R:2 * R])
        base_out[...] = base
        start_out[...] = base.astype(BF16)

    own, peer = (o0, o1, o2, o3), (p0, p1, p2, p3)

    @pl.when(c == 0)
    def _():
        run(own, peer)

    @pl.when(c != 0)
    def _():
        run(peer, own)


def pair_sum(r0, r1, out):
    out[...] = r0[...].astype(F32) + r1[...].astype(F32)


def onward(entry, p_high, p_low, base):
    high, low = halves(entry)
    return base + (nt(high, p_high) + (nt(low, p_high) + nt(high, p_low)))


def hop_block(own, peer, p_high, p_low, base, out):
    out[...] = onward(own[...] + peer[...], p_high[...], p_low[...], base[...]).astype(BF16)


def final_block(own, peer, p_high, p_low, base, message, message_peer, *outs):
    _, v, c, _ = place()
    entry = own[...] + peer[...]
    high, low = halves(entry)
    second = onward(entry, p_high[...], p_low[...], base[...])
    first_block = jnp.where(c == 0, message[...], message_peer[...])
    first = first_block[BLOCK:BLOCK + R, :].astype(F32) + first_block[BLOCK + R:, :].astype(F32)
    first = first - (nt(high, first_block[:BLOCK, :]) + nt(low, first_block[:BLOCK, :]))
    states = jnp.concatenate([first, second], axis=0)
    for d in range(4):
        at = lax.rem(v + d, 4) * CHIP + c * ROWS
        outs[d][...] = pltpu.roll(states, lax.rem(BLOCK - at, BLOCK), 1)[:, :ROWS]


def hop(out):
    arrived = []
    for j in range(2):
        def target(y, x, c, z, j=j):
            y, x, c, _ = along_v(2 * j + c)(y, x, c, z)
            return (y, x, c, z + 1) if z + 1 < Z else None
        arrived.append(send(out, target))
    own = call(pair_sum, shape((R, BLOCK), F32), *arrived)
    return own, to_peer(own)


def local(inverses, lower, forcing, inflow):
    forcing = jnp.swapaxes(forcing, 1, 2)
    inflow = inflow.T
    inverses_peer = to_peer(inverses)
    lower_peer = to_peer(lower)
    inv_own = call(inverse_piece, shape((CHIP, N)), inverses, inverses_peer)
    lower_own = call(hold, shape((ROWS, N)), lower)
    piece = shape((CHIP, BLOCK))
    low = call(
        lower_pieces, [piece] * 4, lower_own, lower_peer,
        scratch=[pltpu.VMEM((CHIP, N), BF16), pltpu.VMEM((4, CHIP, BLOCK), BF16)],
    )
    low = [low[0]] + [send(low[d], along_v(d)) for d in range(1, 4)]
    forcing_peer = to_peer(forcing)
    inflow_peer = to_peer(inflow)
    inv_own, low = lax.optimization_barrier((inv_own, low))
    own = call(
        lower_block, shape((BLOCK + R, BLOCK)), *low, forcing, forcing_peer, inflow, inflow_peer,
        scratch=[pltpu.VMEM((CHIP, LANES), F32)],
    )
    inv_own, own = lax.optimization_barrier((inv_own, own))
    inv = [inv_own] + [send(inv_own, along_v(d)) for d in range(1, 4)]
    inv_panel = call(inverse_panel, shape((BLOCK, N)), *inv)
    panel = [own] + [send(own, along_u(d)) for d in range(1, 4)]

    message = call(
        coupling_block, shape((BLOCK + 2 * R, BLOCK)), inv_panel, *panel,
        scratch=[
            pltpu.VMEM((N, BLOCK), BF16), pltpu.VMEM((N, LANES), BF16), pltpu.VMEM((BLOCK, LANES), BF16),
        ],
        flops=2 * BLOCK * BLOCK * N,
    )
    turn = [message] + [send(message, across(d)) for d in range(1, 4)]
    turn_peer = [to_peer(value) for value in turn]
    p_high, p_low, base, out = call(
        product_block,
        [shape((BLOCK, BLOCK)), shape((BLOCK, BLOCK)), shape((R, BLOCK), F32), shape((R, BLOCK))],
        *turn, *turn_peer,
        scratch=[pltpu.VMEM((BLOCK, N), BF16), pltpu.VMEM((N, BLOCK), BF16), pltpu.VMEM((N, LANES), BF16)],
        flops=2 * BLOCK * BLOCK * N,
    )

    for step in range(Z - 1):
        entry = hop(out)
        if step + 1 < Z - 1:
            out = call(hop_block, shape((R, BLOCK)), *entry, p_high, p_low, base)
    finals = call(
        final_block, [shape((2 * R, ROWS), F32)] * 4, *entry, p_high, p_low, base, turn[0], turn_peer[0]
    )
    total = finals[0]
    for d in range(1, 4):
        total = total + send(finals[d], along_v(d))
    return jnp.swapaxes(total.reshape(2, R, ROWS), 1, 2)


def solution(mesh):
    placed = (
        P("blk", "group", None),
        P("blk", "group", None),
        P("blk", "group", None),
        P("group", None),
    )
    return jax.shard_map(
        local, mesh=mesh, in_specs=placed, out_specs=P("blk", "group", None), check_vma=False
    )
```

```python
import jax
import jax.numpy as jnp
from jax import lax
from jax.experimental import pallas as pl
from jax.experimental.pallas import tpu as pltpu
from jax.sharding import PartitionSpec as P

Y, X, CORES, Z = 4, 4, 2, 4
AXES = ("group", "blk")
ROWS = 48
CHIP = ROWS * CORES
BLOCK = CHIP * X
N = BLOCK * Y
R = 32
LANES = 128
ORDER = (0, 3, 1, 2)
F32, BF16 = jnp.float32, jnp.bfloat16


def send(value, target):
    pairs = []
    for y in range(Y):
        for x in range(X):
            for c in range(CORES):
                for z in range(Z):
                    to = target(y, x, c, z)
                    if to is not None:
                        ty, tx, tc, tz = to
                        pairs.append((
                            ((y * X + x) * CORES + c) * Z + z,
                            ((ty % Y * X + tx % X) * CORES + tc) * Z + tz,
                        ))
    return lax.ppermute(value, AXES, pairs)


def around(value, along):
    return [value] + [send(value, along(d)) for d in ORDER[1:]]


def to_peer(value):
    return send(value, lambda y, x, c, z: (y, x, 1 - c, z))


def along_v(d):
    return lambda y, x, c, z: (y, x + d, c, z) if z % 2 == 0 else (y + d, x, c, z)


def along_u(d):
    return lambda y, x, c, z: (y + d, x, c, z) if z % 2 == 0 else (y, x + d, c, z)


def across(d):
    return lambda y, x, c, z: (along_u(d) if c == 0 else along_v(d))(y, x, c, z)


def place():
    group, z = lax.axis_index("group"), lax.axis_index("blk")
    y, x = group // (X * CORES), (group // CORES) % X
    even = z % 2 == 0
    return jnp.where(even, y, x), jnp.where(even, x, y), group % CORES, z


def chunk(u, v, z):
    return pl.multiple_of(jnp.where(z % 2 == 0, u * BLOCK + v * CHIP, v * BLOCK + u * CHIP), 32)


def rows_at(start, size):
    return pl.ds(pl.multiple_of(start, 16), size)


def lanes_at(start, size):
    return pl.ds(pl.multiple_of(start, 128), size)


def behind(me, d):
    return lax.rem(me - d + 4, 4)


def call(kernel, out, *args, scratch=(), flops=0):
    moved = sum(a.size * a.dtype.itemsize for a in args)
    return pl.pallas_call(
        kernel,
        out_shape=out,
        in_specs=[pl.BlockSpec(memory_space=pltpu.VMEM)] * len(args),
        out_specs=jax.tree.map(lambda _: pl.BlockSpec(memory_space=pltpu.VMEM), out),
        scratch_shapes=list(scratch),
        cost_estimate=pl.CostEstimate(flops=flops, bytes_accessed=moved, transcendentals=0),
        compiler_params=pltpu.CompilerParams(vmem_limit_bytes=24 * 2**20),
    )(*args)


def shape(dims, kind=BF16):
    return jax.ShapeDtypeStruct(dims, kind)


def nt(a, b):
    return lax.dot_general(a, b, (((1,), (1,)), ((), ())), preferred_element_type=F32)


def halves(value):
    high = value.astype(BF16)
    return high, (value - high.astype(F32)).astype(BF16)


def hold(own, out):
    out[...] = own[place()[2]]


def lower_pieces(own, peer, *refs):
    outs, rows, cut = refs[:4], refs[4], refs[5]
    _, v, c, z = place()
    rows[rows_at(c * ROWS, ROWS), :] = own[...]
    rows[rows_at((1 - c) * ROWS, ROWS), :] = peer[c]

    @pl.when(z % 2 == 0)
    def _():
        for b in range(4):
            cut[b] = jnp.concatenate(
                [rows[:, i * BLOCK + b * CHIP:i * BLOCK + (b + 1) * CHIP] for i in range(4)], axis=1
            )

    @pl.when(z % 2 == 1)
    def _():
        for b in range(4):
            cut[b] = rows[:, b * BLOCK:(b + 1) * BLOCK]

    for d in range(4):
        outs[d][...] = cut[lax.rem(v + d, 4)]


def inverse_piece(own, peer, out):
    c = place()[2]
    out[rows_at(c * ROWS, ROWS), :] = own[c]
    out[rows_at((1 - c) * ROWS, ROWS), :] = peer[c]


def inverse_panel(a0, a1, a2, a3, out):
    v = place()[1]
    for d, piece in enumerate((a0, a1, a2, a3)):
        out[rows_at(behind(v, d) * CHIP, CHIP), :] = piece[...]


def lower_block(p0, p1, p2, p3, forcing, forcing_peer, inflow, inflow_peer, out, sides):
    _, v, c, _ = place()
    for d, piece in enumerate((p0, p1, p2, p3)):
        out[rows_at(behind(v, d) * CHIP, CHIP), :] = piece[...]
    for f, e, at in ((forcing, inflow, c * ROWS), (forcing_peer, inflow_peer, (1 - c) * ROWS)):
        high, low = halves(e[...])
        side = jnp.concatenate([f[c].astype(F32), high.astype(F32), low.astype(F32), jnp.zeros((R, ROWS), F32)], axis=0)
        side = jnp.concatenate([side, jnp.zeros((LANES, LANES - ROWS), F32)], axis=1).T
        sides[rows_at(at, ROWS), :] = side[:ROWS]
    for g in range(3):
        out[BLOCK:, g * LANES:(g + 1) * LANES] = sides[g * R:(g + 1) * R, :].astype(BF16)


def coupling_block(panel, l0, l1, l2, l3, out, lower, sides, entry):
    u, v, c, z = place()
    sides[...] = jnp.zeros_like(sides)
    for d, piece in zip(ORDER, (l0, l1, l2, l3)):
        from_u = behind(u, d)
        for j in range(4):
            lower[rows_at(chunk(from_u, j, z), CHIP), :] = piece[j * CHIP:(j + 1) * CHIP, :]
        at = chunk(from_u, v, z)
        for g in range(3):
            part = piece[BLOCK:, g * LANES:(g + 1) * LANES]
            sides[rows_at(at + g * R, R), :] = part
            entry[rows_at(from_u * CHIP + g * R, R), :] = part
    block = jnp.dot(panel[...], lower[...], preferred_element_type=F32).astype(BF16)
    share = jnp.dot(panel[...], sides[...], preferred_element_type=F32)[:, :R]
    known = jnp.dot(block, entry[...], preferred_element_type=F32)
    known = known[:, R:2 * R] + known[:, 2 * R:3 * R]
    share = share - jnp.where((z == 0) & (c == 0), known, 0.0)
    share = jnp.concatenate([share, jnp.zeros((BLOCK, LANES - R), F32)], axis=1).T[:R]
    high, low = halves(share)
    out[:BLOCK, :] = block
    out[BLOCK:BLOCK + R, :] = high
    out[BLOCK + R:, :] = low


def product_block(o0, o1, o2, o3, p0, p1, p2, p3, high_out, low_out, base_out, start_out, second, first, shares):
    u, v, c, _ = place()

    def run(firsts, seconds):
        for d, piece in zip(ORDER, seconds):
            second[:, lanes_at(behind(v, d) * BLOCK, BLOCK)] = piece[:BLOCK, :]
        for d, piece in zip(ORDER, firsts):
            from_u = behind(u, d)
            side = piece[BLOCK:, :].astype(F32)
            side = jnp.concatenate([side, jnp.zeros((LANES - 2 * R, BLOCK), F32)], axis=0).T.astype(BF16)
            for j in range(4):
                at = rows_at(j * BLOCK + from_u * CHIP, CHIP)
                first[at, :] = piece[j * CHIP:(j + 1) * CHIP, :]
                shares[at, :] = side[j * CHIP:(j + 1) * CHIP, :]
        total = jnp.dot(second[...], first[...], preferred_element_type=F32)
        taken = jnp.dot(second[...], shares[...], preferred_element_type=F32).T
        high, low = halves(total)
        high_out[...] = high
        low_out[...] = low
        own = seconds[0][BLOCK:BLOCK + R, :].astype(F32) + seconds[0][BLOCK + R:, :].astype(F32)
        base = own - (taken[:R] + taken[R:2 * R])
        base_out[...] = base
        start_out[...] = base.astype(BF16)

    own, peer = (o0, o1, o2, o3), (p0, p1, p2, p3)

    @pl.when(c == 0)
    def _():
        run(own, peer)

    @pl.when(c != 0)
    def _():
        run(peer, own)


def pair_sum(r0, r1, out):
    out[...] = r0[...].astype(F32) + r1[...].astype(F32)


def onward(entry, p_high, p_low, base):
    high, low = halves(entry)
    return base + (nt(high, p_high) + (nt(low, p_high) + nt(high, p_low)))


def hop_block(own, peer, p_high, p_low, base, out):
    out[...] = onward(own[...] + peer[...], p_high[...], p_low[...], base[...]).astype(BF16)


def final_block(own, peer, p_high, p_low, base, message, message_peer, *outs):
    _, v, c, _ = place()
    entry = own[...] + peer[...]
    high, low = halves(entry)
    second = onward(entry, p_high[...], p_low[...], base[...])
    first_block = jnp.where(c == 0, message[...], message_peer[...])
    first = first_block[BLOCK:BLOCK + R, :].astype(F32) + first_block[BLOCK + R:, :].astype(F32)
    first = first - (nt(high, first_block[:BLOCK, :]) + nt(low, first_block[:BLOCK, :]))
    states = jnp.concatenate([first, second], axis=0)
    for d in range(4):
        at = lax.rem(v + d, 4) * CHIP + c * ROWS
        outs[d][...] = pltpu.roll(states, lax.rem(BLOCK - at, BLOCK), 1)[:, :ROWS]


def hop(out):
    arrived = []
    for j in range(2):
        def target(y, x, c, z, j=j):
            y, x, c, _ = along_v(2 * j + c)(y, x, c, z)
            return (y, x, c, z + 1) if z + 1 < Z else None
        arrived.append(send(out, target))
    own = call(pair_sum, shape((R, BLOCK), F32), *arrived)
    return own, to_peer(own)


def local(inverses, lower, forcing, inflow):
    forcing = jnp.swapaxes(forcing, 1, 2)
    inflow = inflow.T
    inverses_peer = to_peer(inverses)
    lower_peer = to_peer(lower)
    inv_own = call(inverse_piece, shape((CHIP, N)), inverses, inverses_peer)
    lower_own = call(hold, shape((ROWS, N)), lower)
    piece = shape((CHIP, BLOCK))
    low = call(
        lower_pieces, [piece] * 4, lower_own, lower_peer,
        scratch=[pltpu.VMEM((CHIP, N), BF16), pltpu.VMEM((4, CHIP, BLOCK), BF16)],
    )
    low = [low[0]] + [send(low[d], along_v(d)) for d in range(1, 4)]
    forcing_peer = to_peer(forcing)
    inflow_peer = to_peer(inflow)
    inv_own, low[1] = lax.optimization_barrier((inv_own, low[1]))
    inv_2 = send(inv_own, along_v(2))
    own = call(
        lower_block, shape((BLOCK + R, BLOCK)), *low, forcing, forcing_peer, inflow, inflow_peer,
        scratch=[pltpu.VMEM((CHIP, LANES), F32)],
    )
    inv_own, own = lax.optimization_barrier((inv_own, own))
    inv_3, inv_1 = send(inv_own, along_v(3)), send(inv_own, along_v(1))
    inv = [inv_own, inv_1, inv_2, inv_3]
    inv_panel = call(inverse_panel, shape((BLOCK, N)), *inv)
    panel = around(own, along_u)

    message = call(
        coupling_block, shape((BLOCK + 2 * R, BLOCK)), inv_panel, *panel,
        scratch=[
            pltpu.VMEM((N, BLOCK), BF16), pltpu.VMEM((N, LANES), BF16), pltpu.VMEM((BLOCK, LANES), BF16),
        ],
        flops=2 * BLOCK * BLOCK * N,
    )
    turn = around(message, across)
    turn_peer = [to_peer(value) for value in turn]
    p_high, p_low, base, out = call(
        product_block,
        [shape((BLOCK, BLOCK)), shape((BLOCK, BLOCK)), shape((R, BLOCK), F32), shape((R, BLOCK))],
        *turn, *turn_peer,
        scratch=[pltpu.VMEM((BLOCK, N), BF16), pltpu.VMEM((N, BLOCK), BF16), pltpu.VMEM((N, LANES), BF16)],
        flops=2 * BLOCK * BLOCK * N,
    )

    for step in range(Z - 1):
        entry = hop(out)
        if step + 1 < Z - 1:
            out = call(hop_block, shape((R, BLOCK)), *entry, p_high, p_low, base)
    finals = call(
        final_block, [shape((2 * R, ROWS), F32)] * 4, *entry, p_high, p_low, base, turn[0], turn_peer[0]
    )
    total = finals[0]
    for d in range(1, 4):
        total = total + send(finals[d], along_v(d))
    return jnp.swapaxes(total.reshape(2, R, ROWS), 1, 2)


def solution(mesh):
    placed = (
        P("blk", "group", None),
        P("blk", "group", None),
        P("blk", "group", None),
        P("group", None),
    )
    return jax.shard_map(
        local, mesh=mesh, in_specs=placed, out_specs=P("blk", "group", None), check_vma=False
    )
```

```python
import jax
import jax.numpy as jnp
from jax import lax
from jax.experimental import pallas as pl
from jax.experimental.pallas import tpu as pltpu
from jax.sharding import PartitionSpec as P

Y, X, CORES, Z = 4, 4, 2, 4
AXES = ("group", "blk")
ROWS = 48
CHIP = ROWS * CORES
BLOCK = CHIP * X
N = BLOCK * Y
R = 32
LANES = 128
ORDER = (0, 3, 1, 2)
F32, BF16 = jnp.float32, jnp.bfloat16


def send(value, target):
    pairs = []
    for y in range(Y):
        for x in range(X):
            for c in range(CORES):
                for z in range(Z):
                    to = target(y, x, c, z)
                    if to is not None:
                        ty, tx, tc, tz = to
                        pairs.append((
                            ((y * X + x) * CORES + c) * Z + z,
                            ((ty % Y * X + tx % X) * CORES + tc) * Z + tz,
                        ))
    return lax.ppermute(value, AXES, pairs)


def around(value, along):
    return [value] + [send(value, along(d)) for d in ORDER[1:]]


def to_peer(value):
    return send(value, lambda y, x, c, z: (y, x, 1 - c, z))


def along_v(d):
    return lambda y, x, c, z: (y, x + d, c, z) if z % 2 == 0 else (y + d, x, c, z)


def along_u(d):
    return lambda y, x, c, z: (y + d, x, c, z) if z % 2 == 0 else (y, x + d, c, z)


def across(d):
    return lambda y, x, c, z: (along_u(d) if c == 0 else along_v(d))(y, x, c, z)


def place():
    group, z = lax.axis_index("group"), lax.axis_index("blk")
    y, x = group // (X * CORES), (group // CORES) % X
    even = z % 2 == 0
    return jnp.where(even, y, x), jnp.where(even, x, y), group % CORES, z


def chunk(u, v, z):
    return pl.multiple_of(jnp.where(z % 2 == 0, u * BLOCK + v * CHIP, v * BLOCK + u * CHIP), 32)


def rows_at(start, size):
    return pl.ds(pl.multiple_of(start, 16), size)


def lanes_at(start, size):
    return pl.ds(pl.multiple_of(start, 128), size)


def behind(me, d):
    return lax.rem(me - d + 4, 4)


def call(kernel, out, *args, scratch=(), flops=0):
    moved = sum(a.size * a.dtype.itemsize for a in args)
    return pl.pallas_call(
        kernel,
        out_shape=out,
        in_specs=[pl.BlockSpec(memory_space=pltpu.VMEM)] * len(args),
        out_specs=jax.tree.map(lambda _: pl.BlockSpec(memory_space=pltpu.VMEM), out),
        scratch_shapes=list(scratch),
        cost_estimate=pl.CostEstimate(flops=flops, bytes_accessed=moved, transcendentals=0),
        compiler_params=pltpu.CompilerParams(vmem_limit_bytes=24 * 2**20),
    )(*args)


def shape(dims, kind=BF16):
    return jax.ShapeDtypeStruct(dims, kind)


def nt(a, b):
    return lax.dot_general(a, b, (((1,), (1,)), ((), ())), preferred_element_type=F32)


def halves(value):
    high = value.astype(BF16)
    return high, (value - high.astype(F32)).astype(BF16)


def hold(own, out):
    out[...] = own[place()[2]]


def lower_pieces(own, peer, *refs):
    outs, rows, cut = refs[:4], refs[4], refs[5]
    _, v, c, z = place()
    rows[rows_at(c * ROWS, ROWS), :] = own[...]
    rows[rows_at((1 - c) * ROWS, ROWS), :] = peer[c]

    @pl.when(z % 2 == 0)
    def _():
        for b in range(4):
            cut[b] = jnp.concatenate(
                [rows[:, i * BLOCK + b * CHIP:i * BLOCK + (b + 1) * CHIP] for i in range(4)], axis=1
            )

    @pl.when(z % 2 == 1)
    def _():
        for b in range(4):
            cut[b] = rows[:, b * BLOCK:(b + 1) * BLOCK]

    for d in range(4):
        outs[d][...] = cut[lax.rem(v + d, 4)]


def inverse_piece(own, peer, out):
    c = place()[2]
    out[rows_at(c * ROWS, ROWS), :] = own[c]
    out[rows_at((1 - c) * ROWS, ROWS), :] = peer[c]


def inverse_panel(a0, a1, a2, a3, out):
    v = place()[1]
    for d, piece in enumerate((a0, a1, a2, a3)):
        out[rows_at(behind(v, d) * CHIP, CHIP), :] = piece[...]


def lower_block(p0, p1, p2, p3, forcing, forcing_peer, inflow, inflow_peer, out, sides):
    _, v, c, _ = place()
    for d, piece in enumerate((p0, p1, p2, p3)):
        out[rows_at(behind(v, d) * CHIP, CHIP), :] = piece[...]
    for f, e, at in ((forcing, inflow, c * ROWS), (forcing_peer, inflow_peer, (1 - c) * ROWS)):
        high, low = halves(e[...])
        side = jnp.concatenate([f[c].astype(F32), high.astype(F32), low.astype(F32), jnp.zeros((R, ROWS), F32)], axis=0)
        side = jnp.concatenate([side, jnp.zeros((LANES, LANES - ROWS), F32)], axis=1).T
        sides[rows_at(at, ROWS), :] = side[:ROWS]
    for g in range(3):
        out[BLOCK:, g * LANES:(g + 1) * LANES] = sides[g * R:(g + 1) * R, :].astype(BF16)


def coupling_block(panel, l0, l1, l2, l3, out, lower, sides, entry):
    u, v, c, z = place()
    sides[...] = jnp.zeros_like(sides)
    for d, piece in zip(ORDER, (l0, l1, l2, l3)):
        from_u = behind(u, d)
        for j in range(4):
            lower[rows_at(chunk(from_u, j, z), CHIP), :] = piece[j * CHIP:(j + 1) * CHIP, :]
        at = chunk(from_u, v, z)
        for g in range(3):
            part = piece[BLOCK:, g * LANES:(g + 1) * LANES]
            sides[rows_at(at + g * R, R), :] = part
            entry[rows_at(from_u * CHIP + g * R, R), :] = part
    block = jnp.dot(panel[...], lower[...], preferred_element_type=F32).astype(BF16)
    share = jnp.dot(panel[...], sides[...], preferred_element_type=F32)[:, :R]
    known = jnp.dot(block, entry[...], preferred_element_type=F32)
    known = known[:, R:2 * R] + known[:, 2 * R:3 * R]
    share = share - jnp.where((z == 0) & (c == 0), known, 0.0)
    share = jnp.concatenate([share, jnp.zeros((BLOCK, LANES - R), F32)], axis=1).T[:R]
    high, low = halves(share)
    out[:BLOCK, :] = block
    out[BLOCK:BLOCK + R, :] = high
    out[BLOCK + R:, :] = low


def panels(u, v, firsts, seconds, second, first=None, shares=None):
    for d, piece in zip(ORDER, seconds):
        second[:, lanes_at(behind(v, d) * BLOCK, BLOCK)] = piece[:BLOCK, :]
    for d, piece in zip(ORDER, firsts):
        from_u = behind(u, d)
        if shares is not None:
            side = piece[BLOCK:, :].astype(F32)
            side = jnp.concatenate([side, jnp.zeros((LANES - 2 * R, BLOCK), F32)], axis=0).T.astype(BF16)
        for j in range(4):
            at = rows_at(j * BLOCK + from_u * CHIP, CHIP)
            if first is not None:
                first[at, :] = piece[j * CHIP:(j + 1) * CHIP, :]
            if shares is not None:
                shares[at, :] = side[j * CHIP:(j + 1) * CHIP, :]


def base_block(o0, o1, o2, o3, p0, p1, p2, p3, second_out, base_out, start_out, shares):
    u, v, c, _ = place()

    def run(firsts, seconds):
        panels(u, v, firsts, seconds, second_out, shares=shares)
        taken = jnp.dot(second_out[...], shares[...], preferred_element_type=F32).T
        own = seconds[0][BLOCK:BLOCK + R, :].astype(F32) + seconds[0][BLOCK + R:, :].astype(F32)
        base = own - (taken[:R] + taken[R:2 * R])
        base_out[...] = base
        start_out[...] = base.astype(BF16)

    own, peer = (o0, o1, o2, o3), (p0, p1, p2, p3)

    @pl.when(c == 0)
    def _():
        run(own, peer)

    @pl.when(c != 0)
    def _():
        run(peer, own)


def product_block(o0, o1, o2, o3, p0, p1, p2, p3, second, high_out, low_out, first):
    u, v, c, _ = place()
    own, peer = (o0, o1, o2, o3), (p0, p1, p2, p3)

    @pl.when(c == 0)
    def _():
        panels(u, v, own, (), second, first=first)

    @pl.when(c != 0)
    def _():
        panels(u, v, peer, (), second, first=first)

    total = jnp.dot(second[...], first[...], preferred_element_type=F32)
    high, low = halves(total)
    high_out[...] = high
    low_out[...] = low


def pair_sum(r0, r1, out):
    out[...] = r0[...].astype(F32) + r1[...].astype(F32)


def onward(entry, p_high, p_low, base):
    high, low = halves(entry)
    return base + (nt(high, p_high) + (nt(low, p_high) + nt(high, p_low)))


def hop_block(own, peer, p_high, p_low, base, out):
    out[...] = onward(own[...] + peer[...], p_high[...], p_low[...], base[...]).astype(BF16)


def final_block(*refs):
    entries, (p_high, p_low, base, message, message_peer), outs = refs[:6], refs[6:11], refs[11:]
    _, v, c, _ = place()
    entry = sum(e[...] for e in entries)
    high, low = halves(entry)
    second = onward(entry, p_high[...], p_low[...], base[...])
    first_block = jnp.where(c == 0, message[...], message_peer[...])
    first = first_block[BLOCK:BLOCK + R, :].astype(F32) + first_block[BLOCK + R:, :].astype(F32)
    first = first - (nt(high, first_block[:BLOCK, :]) + nt(low, first_block[:BLOCK, :]))
    states = jnp.concatenate([first, second], axis=0)
    for d in range(4):
        at = lax.rem(v + d, 4) * CHIP + c * ROWS
        outs[d][...] = pltpu.roll(states, lax.rem(BLOCK - at, BLOCK), 1)[:, :ROWS]


def hop(out, plane, *beside):
    arrived = []
    for j in range(2):
        def target(y, x, c, z, j=j):
            y, x, c, _ = along_v(2 * j + c)(y, x, c, z)
            return (y, x, c, z + 1) if z + 1 == plane else None
        arrived.append(send(out, target))
    arrived, beside = lax.optimization_barrier((arrived, beside))
    own = call(pair_sum, shape((R, BLOCK), F32), *arrived)
    return (own, to_peer(own)), beside


def local(inverses, lower, forcing, inflow):
    forcing = jnp.swapaxes(forcing, 1, 2)
    inflow = inflow.T
    inverses_peer = to_peer(inverses)
    lower_peer = to_peer(lower)
    inv_own = call(inverse_piece, shape((CHIP, N)), inverses, inverses_peer)
    lower_own = call(hold, shape((ROWS, N)), lower)
    piece = shape((CHIP, BLOCK))
    low = call(
        lower_pieces, [piece] * 4, lower_own, lower_peer,
        scratch=[pltpu.VMEM((CHIP, N), BF16), pltpu.VMEM((4, CHIP, BLOCK), BF16)],
    )
    low = [low[0]] + [send(low[d], along_v(d)) for d in range(1, 4)]
    forcing_peer = to_peer(forcing)
    inflow_peer = to_peer(inflow)
    inv_own, low[1] = lax.optimization_barrier((inv_own, low[1]))
    inv_2 = send(inv_own, along_v(2))
    own = call(
        lower_block, shape((BLOCK + R, BLOCK)), *low, forcing, forcing_peer, inflow, inflow_peer,
        scratch=[pltpu.VMEM((CHIP, LANES), F32)],
    )
    inv_own, own = lax.optimization_barrier((inv_own, own))
    inv_3, inv_1 = send(inv_own, along_v(3)), send(inv_own, along_v(1))
    inv = [inv_own, inv_1, inv_2, inv_3]
    inv_panel = call(inverse_panel, shape((BLOCK, N)), *inv)
    panel = around(own, along_u)

    message = call(
        coupling_block, shape((BLOCK + 2 * R, BLOCK)), inv_panel, *panel,
        scratch=[
            pltpu.VMEM((N, BLOCK), BF16), pltpu.VMEM((N, LANES), BF16), pltpu.VMEM((BLOCK, LANES), BF16),
        ],
        flops=2 * BLOCK * BLOCK * N,
    )
    turn = around(message, across)
    turn_peer = [to_peer(value) for value in turn]
    second, base, out = call(
        base_block, [shape((BLOCK, N)), shape((R, BLOCK), F32), shape((R, BLOCK))], *turn, *turn_peer,
        scratch=[pltpu.VMEM((N, LANES), BF16)],
    )
    p_high, p_low = call(
        product_block, [shape((BLOCK, BLOCK)), shape((BLOCK, BLOCK))], *turn, *turn_peer, second,
        scratch=[pltpu.VMEM((N, BLOCK), BF16)], flops=2 * BLOCK * BLOCK * N,
    )

    entries = []
    for plane in range(1, Z):
        entry, (p_high, p_low) = hop(out, plane, p_high, p_low)
        entries += entry
        if plane + 1 < Z:
            out = call(hop_block, shape((R, BLOCK)), *entry, p_high, p_low, base)
    finals = call(
        final_block, [shape((2 * R, ROWS), F32)] * 4, *entries, p_high, p_low, base, turn[0], turn_peer[0]
    )
    total = finals[0]
    for d in range(1, 4):
        total = total + send(finals[d], along_v(d))
    return jnp.swapaxes(total.reshape(2, R, ROWS), 1, 2)


def solution(mesh):
    placed = (
        P("blk", "group", None),
        P("blk", "group", None),
        P("blk", "group", None),
        P("group", None),
    )
    return jax.shard_map(
        local, mesh=mesh, in_specs=placed, out_specs=P("blk", "group", None), check_vma=False
    )
```

```python
import jax
import jax.numpy as jnp
from jax import lax
from jax.experimental import pallas as pl
from jax.experimental.pallas import tpu as pltpu
from jax.sharding import PartitionSpec as P

Y, X, CORES, Z = 4, 4, 2, 4
AXES = ("group", "blk")
ROWS = 48
CHIP = ROWS * CORES
BLOCK = CHIP * X
N = BLOCK * Y
R = 32
LANES = 128
ORDER = (0, 2, 1, 3)
F32, BF16 = jnp.float32, jnp.bfloat16


def send(value, target):
    pairs = []
    for y in range(Y):
        for x in range(X):
            for c in range(CORES):
                for z in range(Z):
                    to = target(y, x, c, z)
                    if to is not None:
                        ty, tx, tc, tz = to
                        pairs.append((
                            ((y * X + x) * CORES + c) * Z + z,
                            ((ty % Y * X + tx % X) * CORES + tc) * Z + tz,
                        ))
    return lax.ppermute(value, AXES, pairs)


def around(value, along):
    return [value] + [send(value, along(d)) for d in ORDER[1:]]


def to_peer(value):
    return send(value, lambda y, x, c, z: (y, x, 1 - c, z))


def along_v(d):
    return lambda y, x, c, z: (y, x + d, c, z) if z % 2 == 0 else (y + d, x, c, z)


def along_u(d):
    return lambda y, x, c, z: (y + d, x, c, z) if z % 2 == 0 else (y, x + d, c, z)


def across(d):
    return lambda y, x, c, z: (along_u(d) if c == 0 else along_v(d))(y, x, c, z)


def place():
    group, z = lax.axis_index("group"), lax.axis_index("blk")
    y, x = group // (X * CORES), (group // CORES) % X
    even = z % 2 == 0
    return jnp.where(even, y, x), jnp.where(even, x, y), group % CORES, z


def chunk(u, v, z):
    return pl.multiple_of(jnp.where(z % 2 == 0, u * BLOCK + v * CHIP, v * BLOCK + u * CHIP), 32)


def rows_at(start, size):
    return pl.ds(pl.multiple_of(start, 16), size)


def lanes_at(start, size):
    return pl.ds(pl.multiple_of(start, 128), size)


def behind(me, d):
    return lax.rem(me - d + 4, 4)


def call(kernel, out, *args, scratch=(), flops=0):
    moved = sum(a.size * a.dtype.itemsize for a in args)
    return pl.pallas_call(
        kernel,
        out_shape=out,
        in_specs=[pl.BlockSpec(memory_space=pltpu.VMEM)] * len(args),
        out_specs=jax.tree.map(lambda _: pl.BlockSpec(memory_space=pltpu.VMEM), out),
        scratch_shapes=list(scratch),
        cost_estimate=pl.CostEstimate(flops=flops, bytes_accessed=moved, transcendentals=0),
        compiler_params=pltpu.CompilerParams(vmem_limit_bytes=24 * 2**20),
    )(*args)


def shape(dims, kind=BF16):
    return jax.ShapeDtypeStruct(dims, kind)


def nt(a, b):
    return lax.dot_general(a, b, (((1,), (1,)), ((), ())), preferred_element_type=F32)


def halves(value):
    high = value.astype(BF16)
    return high, (value - high.astype(F32)).astype(BF16)


def hold(own, out):
    out[...] = own[place()[2]]


def lower_pieces(own, peer, *refs):
    outs, rows, cut = refs[:4], refs[4], refs[5]
    _, v, c, z = place()
    rows[rows_at(c * ROWS, ROWS), :] = own[...]
    rows[rows_at((1 - c) * ROWS, ROWS), :] = peer[c]

    @pl.when(z % 2 == 0)
    def _():
        for b in range(4):
            cut[b] = jnp.concatenate(
                [rows[:, i * BLOCK + b * CHIP:i * BLOCK + (b + 1) * CHIP] for i in range(4)], axis=1
            )

    @pl.when(z % 2 == 1)
    def _():
        for b in range(4):
            cut[b] = rows[:, b * BLOCK:(b + 1) * BLOCK]

    for d in range(4):
        outs[d][...] = cut[lax.rem(v + d, 4)]


def inverse_piece(own, peer, out):
    c = place()[2]
    out[rows_at(c * ROWS, ROWS), :] = own[c]
    out[rows_at((1 - c) * ROWS, ROWS), :] = peer[c]


def inverse_panel(a0, a3, a2, a1, out):
    v = place()[1]
    for d, piece in enumerate((a0, a1, a2, a3)):
        out[rows_at(behind(v, d) * CHIP, CHIP), :] = piece[...]


def lower_block(p0, p1, p2, p3, forcing, forcing_peer, inflow, inflow_peer, out, sides):
    _, v, c, _ = place()
    for d, piece in enumerate((p0, p1, p2, p3)):
        out[rows_at(behind(v, d) * CHIP, CHIP), :] = piece[...]
    for f, e, at in ((forcing, inflow, c * ROWS), (forcing_peer, inflow_peer, (1 - c) * ROWS)):
        high, low = halves(e[...])
        side = jnp.concatenate([f[c].astype(F32), high.astype(F32), low.astype(F32), jnp.zeros((R, ROWS), F32)], axis=0)
        side = jnp.concatenate([side, jnp.zeros((LANES, LANES - ROWS), F32)], axis=1).T
        sides[rows_at(at, ROWS), :] = side[:ROWS]
    for g in range(3):
        out[BLOCK:, g * LANES:(g + 1) * LANES] = sides[g * R:(g + 1) * R, :].astype(BF16)


def coupling_block(panel, l0, l1, l2, l3, out, lower, sides, entry):
    u, v, c, z = place()
    sides[...] = jnp.zeros_like(sides)
    for d, piece in zip(ORDER, (l0, l1, l2, l3)):
        from_u = behind(u, d)
        for j in range(4):
            lower[rows_at(chunk(from_u, j, z), CHIP), :] = piece[j * CHIP:(j + 1) * CHIP, :]
        at = chunk(from_u, v, z)
        for g in range(3):
            part = piece[BLOCK:, g * LANES:(g + 1) * LANES]
            sides[rows_at(at + g * R, R), :] = part
            entry[rows_at(from_u * CHIP + g * R, R), :] = part
    block = jnp.dot(panel[...], lower[...], preferred_element_type=F32).astype(BF16)
    share = jnp.dot(panel[...], sides[...], preferred_element_type=F32)[:, :R]
    known = jnp.dot(block, entry[...], preferred_element_type=F32)
    known = known[:, R:2 * R] + known[:, 2 * R:3 * R]
    share = share - jnp.where((z == 0) & (c == 0), known, 0.0)
    share = jnp.concatenate([share, jnp.zeros((BLOCK, LANES - R), F32)], axis=1).T[:R]
    out[:BLOCK, :] = block
    out[BLOCK:, :] = share.astype(BF16)


def panels(u, v, firsts, seconds, second, first=None, shares=None):
    for d, piece in zip(ORDER, seconds):
        second[:, lanes_at(behind(v, d) * BLOCK, BLOCK)] = piece[:BLOCK, :]
    for d, piece in zip(ORDER, firsts):
        from_u = behind(u, d)
        if shares is not None:
            side = piece[BLOCK:, :].astype(F32)
            side = jnp.concatenate([side, jnp.zeros((LANES - R, BLOCK), F32)], axis=0).T.astype(BF16)
        for j in range(4):
            at = rows_at(j * BLOCK + from_u * CHIP, CHIP)
            if first is not None:
                first[at, :] = piece[j * CHIP:(j + 1) * CHIP, :]
            if shares is not None:
                shares[at, :] = side[j * CHIP:(j + 1) * CHIP, :]


def base_block(o0, o1, o2, o3, p0, p1, p2, p3, second_out, base_out, start_out, shares):
    u, v, c, _ = place()

    def run(firsts, seconds):
        panels(u, v, firsts, seconds, second_out, shares=shares)
        taken = jnp.dot(second_out[...], shares[...], preferred_element_type=F32).T
        base = seconds[0][BLOCK:, :].astype(F32) - taken[:R]
        base_out[...] = base
        start_out[...] = base.astype(BF16)

    own, peer = (o0, o1, o2, o3), (p0, p1, p2, p3)

    @pl.when(c == 0)
    def _():
        run(own, peer)

    @pl.when(c != 0)
    def _():
        run(peer, own)


def product_block(o0, o1, o2, o3, p0, p1, p2, p3, second, high_out, low_out, first):
    u, v, c, _ = place()
    own, peer = (o0, o1, o2, o3), (p0, p1, p2, p3)

    @pl.when(c == 0)
    def _():
        panels(u, v, own, (), second, first=first)

    @pl.when(c != 0)
    def _():
        panels(u, v, peer, (), second, first=first)

    total = jnp.dot(second[...], first[...], preferred_element_type=F32)
    high, low = halves(total)
    high_out[...] = high
    low_out[...] = low


def pair_sum(r0, r1, out):
    out[...] = r0[...].astype(F32) + r1[...].astype(F32)


def onward(entry, p_high, p_low, base):
    high, low = halves(entry)
    return base + (nt(high, p_high) + (nt(low, p_high) + nt(high, p_low)))


def hop_block(own, peer, p_high, p_low, base, out):
    out[...] = onward(own[...] + peer[...], p_high[...], p_low[...], base[...]).astype(BF16)


def final_block(*refs):
    entries, (p_high, p_low, base, message, message_peer), outs = refs[:6], refs[6:11], refs[11:]
    _, v, c, _ = place()
    entry = sum(e[...] for e in entries)
    high, low = halves(entry)
    second = onward(entry, p_high[...], p_low[...], base[...])
    first_block = jnp.where(c == 0, message[...], message_peer[...])
    first = first_block[BLOCK:, :].astype(F32) - (nt(high, first_block[:BLOCK, :]) + nt(low, first_block[:BLOCK, :]))
    states = jnp.concatenate([first, second], axis=0)
    for d in range(4):
        at = lax.rem(v + d, 4) * CHIP + c * ROWS
        outs[d][...] = pltpu.roll(states, lax.rem(BLOCK - at, BLOCK), 1)[:, :ROWS]


def hop(out, plane, *beside):
    arrived = []
    for j in range(2):
        def target(y, x, c, z, j=j):
            y, x, c, _ = along_v(2 * j + c)(y, x, c, z)
            return (y, x, c, z + 1) if z + 1 == plane else None
        arrived.append(send(out, target))
    arrived, beside = lax.optimization_barrier((arrived, beside))
    own = call(pair_sum, shape((R, BLOCK), F32), *arrived)
    return (own, to_peer(own)), beside


def local(inverses, lower, forcing, inflow):
    forcing = jnp.swapaxes(forcing, 1, 2)
    inflow = inflow.T
    inverses_peer = to_peer(inverses)
    lower_peer = to_peer(lower)
    inv_own = call(inverse_piece, shape((CHIP, N)), inverses, inverses_peer)
    lower_own = call(hold, shape((ROWS, N)), lower)
    piece = shape((CHIP, BLOCK))
    low = call(
        lower_pieces, [piece] * 4, lower_own, lower_peer,
        scratch=[pltpu.VMEM((CHIP, N), BF16), pltpu.VMEM((4, CHIP, BLOCK), BF16)],
    )
    low = [low[0]] + [send(low[d], along_v(d)) for d in range(1, 4)]
    forcing_peer = to_peer(forcing)
    inflow_peer = to_peer(inflow)
    inv_own, low[1] = lax.optimization_barrier((inv_own, low[1]))
    inv_2 = send(inv_own, along_v(2))
    own = call(
        lower_block, shape((BLOCK + R, BLOCK)), *low, forcing, forcing_peer, inflow, inflow_peer,
        scratch=[pltpu.VMEM((CHIP, LANES), F32)],
    )
    inv_own, own = lax.optimization_barrier((inv_own, own))
    inv_3, inv_1 = send(inv_own, along_v(3)), send(inv_own, along_v(1))
    inv = [inv_own, inv_3, inv_2, inv_1]
    inv_panel = call(inverse_panel, shape((BLOCK, N)), *inv)
    panel = around(own, along_u)

    message = call(
        coupling_block, shape((BLOCK + R, BLOCK)), inv_panel, *panel,
        scratch=[
            pltpu.VMEM((N, BLOCK), BF16), pltpu.VMEM((N, LANES), BF16), pltpu.VMEM((BLOCK, LANES), BF16),
        ],
        flops=2 * BLOCK * BLOCK * N,
    )
    turn = around(message, across)
    turn_peer = [to_peer(value) for value in turn]
    second, base, out = call(
        base_block, [shape((BLOCK, N)), shape((R, BLOCK), F32), shape((R, BLOCK))], *turn, *turn_peer,
        scratch=[pltpu.VMEM((N, LANES), BF16)],
    )
    p_high, p_low = call(
        product_block, [shape((BLOCK, BLOCK)), shape((BLOCK, BLOCK))], *turn, *turn_peer, second,
        scratch=[pltpu.VMEM((N, BLOCK), BF16)], flops=2 * BLOCK * BLOCK * N,
    )

    entries = []
    for plane in range(1, Z):
        entry, (p_high, p_low) = hop(out, plane, p_high, p_low)
        entries += entry
        if plane + 1 < Z:
            out = call(hop_block, shape((R, BLOCK)), *entry, p_high, p_low, base)
    finals = call(
        final_block, [shape((2 * R, ROWS), F32)] * 4, *entries, p_high, p_low, base, turn[0], turn_peer[0]
    )
    total = finals[0]
    for d in range(1, 4):
        total = total + send(finals[d], along_v(d))
    return jnp.swapaxes(total.reshape(2, R, ROWS), 1, 2)


def solution(mesh):
    placed = (
        P("blk", "group", None),
        P("blk", "group", None),
        P("blk", "group", None),
        P("group", None),
    )
    return jax.shard_map(
        local, mesh=mesh, in_specs=placed, out_specs=P("blk", "group", None), check_vma=False
    )
```

```python
import jax
import jax.numpy as jnp
from jax import lax
from jax.experimental import pallas as pl
from jax.experimental.pallas import tpu as pltpu
from jax.sharding import PartitionSpec as P

Y, X, CORES, Z = 4, 4, 2, 4
AXES = ("group", "blk")
ROWS = 48
CHIP = ROWS * CORES
BLOCK = CHIP * X
N = BLOCK * Y
R = 32
LANES = 128
LOWER_ORDER = (0, 2, 1, 3)
TURN_ORDER = (0, 3, 1, 2)
F32, BF16 = jnp.float32, jnp.bfloat16


def send(value, target):
    pairs = []
    for y in range(Y):
        for x in range(X):
            for c in range(CORES):
                for z in range(Z):
                    to = target(y, x, c, z)
                    if to is not None:
                        ty, tx, tc, tz = to
                        pairs.append((
                            ((y * X + x) * CORES + c) * Z + z,
                            ((ty % Y * X + tx % X) * CORES + tc) * Z + tz,
                        ))
    return lax.ppermute(value, AXES, pairs)


def around(value, along, order):
    return [value] + [send(value, along(d)) for d in order[1:]]


def to_peer(value):
    return send(value, lambda y, x, c, z: (y, x, 1 - c, z))


def along_v(d):
    return lambda y, x, c, z: (y, x + d, c, z) if z % 2 == 0 else (y + d, x, c, z)


def along_u(d):
    return lambda y, x, c, z: (y + d, x, c, z) if z % 2 == 0 else (y, x + d, c, z)


def across(d):
    return lambda y, x, c, z: (along_u(d) if c == 0 else along_v(d))(y, x, c, z)


def place():
    group, z = lax.axis_index("group"), lax.axis_index("blk")
    y, x = group // (X * CORES), (group // CORES) % X
    even = z % 2 == 0
    return jnp.where(even, y, x), jnp.where(even, x, y), group % CORES, z


def chunk(u, v, z):
    return pl.multiple_of(jnp.where(z % 2 == 0, u * BLOCK + v * CHIP, v * BLOCK + u * CHIP), 32)


def rows_at(start, size):
    return pl.ds(pl.multiple_of(start, 16), size)


def lanes_at(start, size):
    return pl.ds(pl.multiple_of(start, 128), size)


def behind(me, d):
    return lax.rem(me - d + 4, 4)


def call(kernel, out, *args, scratch=(), flops=0):
    moved = sum(a.size * a.dtype.itemsize for a in args)
    return pl.pallas_call(
        kernel,
        out_shape=out,
        in_specs=[pl.BlockSpec(memory_space=pltpu.VMEM)] * len(args),
        out_specs=jax.tree.map(lambda _: pl.BlockSpec(memory_space=pltpu.VMEM), out),
        scratch_shapes=list(scratch),
        cost_estimate=pl.CostEstimate(flops=flops, bytes_accessed=moved, transcendentals=0),
        compiler_params=pltpu.CompilerParams(vmem_limit_bytes=24 * 2**20),
    )(*args)


def shape(dims, kind=BF16):
    return jax.ShapeDtypeStruct(dims, kind)


def nt(a, b):
    return lax.dot_general(a, b, (((1,), (1,)), ((), ())), preferred_element_type=F32)


def halves(value):
    high = value.astype(BF16)
    return high, (value - high.astype(F32)).astype(BF16)


def hold(own, out):
    out[...] = own[place()[2]]


def lower_pieces(own, peer, *refs):
    outs, rows, cut = refs[:4], refs[4], refs[5]
    _, v, c, z = place()
    rows[rows_at(c * ROWS, ROWS), :] = own[...]
    rows[rows_at((1 - c) * ROWS, ROWS), :] = peer[c]

    @pl.when(z % 2 == 0)
    def _():
        for b in range(4):
            cut[b] = jnp.concatenate(
                [rows[:, i * BLOCK + b * CHIP:i * BLOCK + (b + 1) * CHIP] for i in range(4)], axis=1
            )

    @pl.when(z % 2 == 1)
    def _():
        for b in range(4):
            cut[b] = rows[:, b * BLOCK:(b + 1) * BLOCK]

    for d in range(4):
        outs[d][...] = cut[lax.rem(v + d, 4)]


def inverse_piece(own, peer, out):
    c = place()[2]
    out[rows_at(c * ROWS, ROWS), :] = own[c]
    out[rows_at((1 - c) * ROWS, ROWS), :] = peer[c]


def lower_block(p0, p1, p2, p3, forcing, forcing_peer, inflow, inflow_peer, out, sides):
    _, v, c, _ = place()
    for d, piece in enumerate((p0, p1, p2, p3)):
        out[rows_at(behind(v, d) * CHIP, CHIP), :] = piece[...]
    for f, e, at in ((forcing, inflow, c * ROWS), (forcing_peer, inflow_peer, (1 - c) * ROWS)):
        high, low = halves(e[...])
        side = jnp.concatenate([f[c].astype(F32), high.astype(F32), low.astype(F32), jnp.zeros((R, ROWS), F32)], axis=0)
        side = jnp.concatenate([side, jnp.zeros((LANES, LANES - ROWS), F32)], axis=1).T
        sides[rows_at(at, ROWS), :] = side[:ROWS]
    for g in range(3):
        out[BLOCK:, g * LANES:(g + 1) * LANES] = sides[g * R:(g + 1) * R, :].astype(BF16)


def coupling_block(a0, a3, a2, a1, l0, l1, l2, l3, out, panel, lower, entry):
    u, v, c, z = place()
    lower[:, BLOCK:] = jnp.zeros((N, LANES), BF16)
    for d, piece in enumerate((a0, a1, a2, a3)):
        panel[rows_at(behind(v, d) * CHIP, CHIP), :] = piece[...]
    for d, piece in zip(LOWER_ORDER, (l0, l1, l2, l3)):
        from_u = behind(u, d)
        for j in range(4):
            lower[rows_at(chunk(from_u, j, z), CHIP), :BLOCK] = piece[j * CHIP:(j + 1) * CHIP, :]
        at = chunk(from_u, v, z)
        for g in range(3):
            part = piece[BLOCK:, g * LANES:(g + 1) * LANES]
            lower[rows_at(at + g * R, R), BLOCK:] = part
            entry[rows_at(from_u * CHIP + g * R, R), :] = part
    both = jnp.dot(panel[...], lower[...], preferred_element_type=F32)
    block = both[:, :BLOCK].astype(BF16)
    share = both[:, BLOCK:BLOCK + R]
    known = jnp.dot(block, entry[...], preferred_element_type=F32)
    known = known[:, R:2 * R] + known[:, 2 * R:3 * R]
    share = share - jnp.where((z == 0) & (c == 0), known, 0.0)
    share = jnp.concatenate([share, jnp.zeros((BLOCK, LANES - R), F32)], axis=1).T[:R]
    out[:BLOCK, :] = block
    out[BLOCK:, :] = share.astype(BF16)


def panels(u, v, firsts, seconds, second, first=None, shares=None):
    for d, piece in zip(TURN_ORDER, seconds):
        second[:, lanes_at(behind(v, d) * BLOCK, BLOCK)] = piece[:BLOCK, :]
    for d, piece in zip(TURN_ORDER, firsts):
        from_u = behind(u, d)
        if shares is not None:
            side = piece[BLOCK:, :].astype(F32)
            side = jnp.concatenate([side, jnp.zeros((LANES - R, BLOCK), F32)], axis=0).T.astype(BF16)
        for j in range(4):
            at = rows_at(j * BLOCK + from_u * CHIP, CHIP)
            if first is not None:
                first[at, :] = piece[j * CHIP:(j + 1) * CHIP, :]
            if shares is not None:
                shares[at, :] = side[j * CHIP:(j + 1) * CHIP, :]


def base_block(o0, o1, o2, o3, p0, p1, p2, p3, second_out, base_out, start_out, shares):
    u, v, c, _ = place()

    def run(firsts, seconds):
        panels(u, v, firsts, seconds, second_out, shares=shares)
        taken = jnp.dot(second_out[...], shares[...], preferred_element_type=F32).T
        base = seconds[0][BLOCK:, :].astype(F32) - taken[:R]
        base_out[...] = base
        start_out[...] = base.astype(BF16)

    own, peer = (o0, o1, o2, o3), (p0, p1, p2, p3)

    @pl.when(c == 0)
    def _():
        run(own, peer)

    @pl.when(c != 0)
    def _():
        run(peer, own)


def product_block(o0, o1, o2, o3, p0, p1, p2, p3, second, high_out, low_out, first):
    u, v, c, _ = place()
    own, peer = (o0, o1, o2, o3), (p0, p1, p2, p3)

    @pl.when(c == 0)
    def _():
        panels(u, v, own, (), second, first=first)

    @pl.when(c != 0)
    def _():
        panels(u, v, peer, (), second, first=first)

    total = jnp.dot(second[...], first[...], preferred_element_type=F32)
    high, low = halves(total)
    high_out[...] = high
    low_out[...] = low


def pair_sum(r0, r1, out):
    out[...] = r0[...].astype(F32) + r1[...].astype(F32)


def onward(entry, p_high, p_low, base):
    high, low = halves(entry)
    return base + (nt(high, p_high) + (nt(low, p_high) + nt(high, p_low)))


def hop_block(own, peer, p_high, p_low, base, out):
    out[...] = onward(own[...] + peer[...], p_high[...], p_low[...], base[...]).astype(BF16)


def final_block(*refs):
    entries, (p_high, p_low, base, message, message_peer), outs = refs[:6], refs[6:11], refs[11:]
    _, v, c, _ = place()
    entry = sum(e[...] for e in entries)
    high, low = halves(entry)
    second = onward(entry, p_high[...], p_low[...], base[...])
    first_block = jnp.where(c == 0, message[...], message_peer[...])
    first = first_block[BLOCK:, :].astype(F32) - (nt(high, first_block[:BLOCK, :]) + nt(low, first_block[:BLOCK, :]))
    states = jnp.concatenate([first, second], axis=0)
    for d in range(4):
        at = lax.rem(v + d, 4) * CHIP + c * ROWS
        outs[d][...] = pltpu.roll(states, lax.rem(BLOCK - at, BLOCK), 1)[:, :ROWS]


def hop(out, plane, *beside):
    arrived = []
    for j in range(2):
        def target(y, x, c, z, j=j):
            y, x, c, _ = along_v(2 * j + c)(y, x, c, z)
            return (y, x, c, z + 1) if z + 1 == plane else None
        arrived.append(send(out, target))
    arrived, beside = lax.optimization_barrier((arrived, beside))
    own = call(pair_sum, shape((R, BLOCK), F32), *arrived)
    return (own, to_peer(own)), beside


def local(inverses, lower, forcing, inflow):
    forcing = jnp.swapaxes(forcing, 1, 2)
    inflow = inflow.T
    inverses_peer = to_peer(inverses)
    lower_peer = to_peer(lower)
    inv_own = call(inverse_piece, shape((CHIP, N)), inverses, inverses_peer)
    lower_own = call(hold, shape((ROWS, N)), lower)
    piece = shape((CHIP, BLOCK))
    low = call(
        lower_pieces, [piece] * 4, lower_own, lower_peer,
        scratch=[pltpu.VMEM((CHIP, N), BF16), pltpu.VMEM((4, CHIP, BLOCK), BF16)],
    )
    low = [low[0]] + [send(low[d], along_v(d)) for d in range(1, 4)]
    forcing_peer = to_peer(forcing)
    inflow_peer = to_peer(inflow)
    inv_own, low[1] = lax.optimization_barrier((inv_own, low[1]))
    inv_2 = send(inv_own, along_v(2))
    own = call(
        lower_block, shape((BLOCK + R, BLOCK)), *low, forcing, forcing_peer, inflow, inflow_peer,
        scratch=[pltpu.VMEM((CHIP, LANES), F32)],
    )
    inv_own, own = lax.optimization_barrier((inv_own, own))
    inv_3, inv_1 = send(inv_own, along_v(3)), send(inv_own, along_v(1))
    inv = [inv_own, inv_3, inv_2, inv_1]
    panel = around(own, along_u, LOWER_ORDER)

    message = call(
        coupling_block, shape((BLOCK + R, BLOCK)), *inv, *panel,
        scratch=[
            pltpu.VMEM((BLOCK, N), BF16), pltpu.VMEM((N, BLOCK + LANES), BF16), pltpu.VMEM((BLOCK, LANES), BF16),
        ],
        flops=2 * BLOCK * BLOCK * N,
    )
    turn = around(message, across, TURN_ORDER)
    turn_peer = [to_peer(value) for value in turn]
    second, base, out = call(
        base_block, [shape((BLOCK, N)), shape((R, BLOCK), F32), shape((R, BLOCK))], *turn, *turn_peer,
        scratch=[pltpu.VMEM((N, LANES), BF16)],
    )
    p_high, p_low = call(
        product_block, [shape((BLOCK, BLOCK)), shape((BLOCK, BLOCK))], *turn, *turn_peer, second,
        scratch=[pltpu.VMEM((N, BLOCK), BF16)], flops=2 * BLOCK * BLOCK * N,
    )

    entries = []
    for plane in range(1, Z):
        entry, (p_high, p_low) = hop(out, plane, p_high, p_low)
        entries += entry
        if plane + 1 < Z:
            out = call(hop_block, shape((R, BLOCK)), *entry, p_high, p_low, base)
    finals = call(
        final_block, [shape((2 * R, ROWS), F32)] * 4, *entries, p_high, p_low, base, turn[0], turn_peer[0]
    )
    total = finals[0]
    for d in range(1, 4):
        total = total + send(finals[d], along_v(d))
    return jnp.swapaxes(total.reshape(2, R, ROWS), 1, 2)


def solution(mesh):
    placed = (
        P("blk", "group", None),
        P("blk", "group", None),
        P("blk", "group", None),
        P("group", None),
    )
    return jax.shard_map(
        local, mesh=mesh, in_specs=placed, out_specs=P("blk", "group", None), check_vma=False
    )
```

```python
import jax
import jax.numpy as jnp
from jax import lax
from jax.experimental import pallas as pl
from jax.experimental.pallas import tpu as pltpu
from jax.sharding import PartitionSpec as P

Y, X, CORES, Z = 4, 4, 2, 4
AXES = ("group", "blk")
ROWS = 48
CHIP = ROWS * CORES
BLOCK = CHIP * X
N = BLOCK * Y
R = 32
LANES = 128
LOWER_ORDER = (0, 2, 1, 3)
TURN_ORDER = (0, 3, 1, 2)
F32, BF16 = jnp.float32, jnp.bfloat16


def send(value, target):
    pairs = []
    for y in range(Y):
        for x in range(X):
            for c in range(CORES):
                for z in range(Z):
                    to = target(y, x, c, z)
                    if to is not None:
                        ty, tx, tc, tz = to
                        pairs.append((
                            ((y * X + x) * CORES + c) * Z + z,
                            ((ty % Y * X + tx % X) * CORES + tc) * Z + tz,
                        ))
    return lax.ppermute(value, AXES, pairs)


def around(value, along, order):
    return [value] + [send(value, along(d)) for d in order[1:]]


def to_peer(value):
    return send(value, lambda y, x, c, z: (y, x, 1 - c, z))


def along_v(d):
    return lambda y, x, c, z: (y, x + d, c, z) if z % 2 == 0 else (y + d, x, c, z)


def along_u(d):
    return lambda y, x, c, z: (y + d, x, c, z) if z % 2 == 0 else (y, x + d, c, z)


def across(d):
    return lambda y, x, c, z: (along_u(d) if c == 0 else along_v(d))(y, x, c, z)


def place():
    group, z = lax.axis_index("group"), lax.axis_index("blk")
    y, x = group // (X * CORES), (group // CORES) % X
    even = z % 2 == 0
    return jnp.where(even, y, x), jnp.where(even, x, y), group % CORES, z


def chunk(u, v, z):
    return pl.multiple_of(jnp.where(z % 2 == 0, u * BLOCK + v * CHIP, v * BLOCK + u * CHIP), 32)


def rows_at(start, size):
    return pl.ds(pl.multiple_of(start, 16), size)


def lanes_at(start, size):
    return pl.ds(pl.multiple_of(start, 128), size)


def behind(me, d):
    return lax.rem(me - d + 4, 4)


def call(kernel, out, *args, scratch=(), flops=0):
    moved = sum(a.size * a.dtype.itemsize for a in args)
    return pl.pallas_call(
        kernel,
        out_shape=out,
        in_specs=[pl.BlockSpec(memory_space=pltpu.VMEM)] * len(args),
        out_specs=jax.tree.map(lambda _: pl.BlockSpec(memory_space=pltpu.VMEM), out),
        scratch_shapes=list(scratch),
        cost_estimate=pl.CostEstimate(flops=flops, bytes_accessed=moved, transcendentals=0),
        compiler_params=pltpu.CompilerParams(vmem_limit_bytes=24 * 2**20),
    )(*args)


def shape(dims, kind=BF16):
    return jax.ShapeDtypeStruct(dims, kind)


def nt(a, b):
    return lax.dot_general(a, b, (((1,), (1,)), ((), ())), preferred_element_type=F32)


def halves(value):
    high = value.astype(BF16)
    return high, (value - high.astype(F32)).astype(BF16)


def hold(own, out):
    out[...] = own[place()[2]]


def lower_pieces(own, peer, *refs):
    outs, rows, cut = refs[:4], refs[4], refs[5]
    _, v, c, z = place()
    rows[rows_at(c * ROWS, ROWS), :] = own[...]
    rows[rows_at((1 - c) * ROWS, ROWS), :] = peer[c]

    @pl.when(z % 2 == 0)
    def _():
        for b in range(4):
            cut[b] = jnp.concatenate(
                [rows[:, i * BLOCK + b * CHIP:i * BLOCK + (b + 1) * CHIP] for i in range(4)], axis=1
            )

    @pl.when(z % 2 == 1)
    def _():
        for b in range(4):
            cut[b] = rows[:, b * BLOCK:(b + 1) * BLOCK]

    for d in range(4):
        outs[d][...] = cut[lax.rem(v + d, 4)]


def inverse_piece(own, peer, out):
    c = place()[2]
    out[rows_at(c * ROWS, ROWS), :] = own[c]
    out[rows_at((1 - c) * ROWS, ROWS), :] = peer[c]


def lower_block(p0, p1, p2, p3, forcing, forcing_peer, inflow, inflow_peer, out, sides):
    _, v, c, _ = place()
    for d, piece in enumerate((p0, p1, p2, p3)):
        out[rows_at(behind(v, d) * CHIP, CHIP), :] = piece[...]
    for f, e, at in ((forcing, inflow, c * ROWS), (forcing_peer, inflow_peer, (1 - c) * ROWS)):
        high, low = halves(e[...])
        side = jnp.concatenate([f[c].astype(F32), high.astype(F32), low.astype(F32), jnp.zeros((R, ROWS), F32)], axis=0)
        side = jnp.concatenate([side, jnp.zeros((LANES, LANES - ROWS), F32)], axis=1).T
        sides[rows_at(at, ROWS), :] = side[:ROWS]
    for g in range(3):
        out[BLOCK:, g * LANES:(g + 1) * LANES] = sides[g * R:(g + 1) * R, :].astype(BF16)


def coupling_block(a0, a3, a2, a1, l0, l1, l2, l3, out, panel, lower, entry):
    u, v, c, z = place()
    lower[:, BLOCK:] = jnp.zeros((N, LANES), BF16)
    for d, piece in enumerate((a0, a1, a2, a3)):
        panel[rows_at(behind(v, d) * CHIP, CHIP), :] = piece[...]
    for d, piece in zip(LOWER_ORDER, (l0, l1, l2, l3)):
        from_u = behind(u, d)
        for j in range(4):
            lower[rows_at(chunk(from_u, j, z), CHIP), :BLOCK] = piece[j * CHIP:(j + 1) * CHIP, :]
        at = chunk(from_u, v, z)
        for g in range(3):
            part = piece[BLOCK:, g * LANES:(g + 1) * LANES]
            lower[rows_at(at + g * R, R), BLOCK:] = part
            entry[rows_at(from_u * CHIP + g * R, R), :] = part
    both = jnp.dot(panel[...], lower[...], preferred_element_type=F32)
    block = both[:, :BLOCK].astype(BF16)
    share = both[:, BLOCK:BLOCK + R]
    known = jnp.dot(block, entry[...], preferred_element_type=F32)
    known = known[:, R:2 * R] + known[:, 2 * R:3 * R]
    share = share - jnp.where((z == 0) & (c == 0), known, 0.0)
    share = jnp.concatenate([share, jnp.zeros((BLOCK, LANES - R), F32)], axis=1).T[:R]
    out[:BLOCK, :] = block
    out[BLOCK:, :] = share.astype(BF16)


def panels(u, v, firsts, seconds, second, first=None, shares=None):
    for d, piece in zip(TURN_ORDER, seconds):
        second[:, lanes_at(behind(v, d) * BLOCK, BLOCK)] = piece[:BLOCK, :]
    for d, piece in zip(TURN_ORDER, firsts):
        from_u = behind(u, d)
        if shares is not None:
            side = piece[BLOCK:, :].astype(F32)
            side = jnp.concatenate([side, jnp.zeros((LANES - R, BLOCK), F32)], axis=0).T.astype(BF16)
        for j in range(4):
            at = rows_at(j * BLOCK + from_u * CHIP, CHIP)
            if first is not None:
                first[at, :] = piece[j * CHIP:(j + 1) * CHIP, :]
            if shares is not None:
                shares[at, :] = side[j * CHIP:(j + 1) * CHIP, :]


def base_block(o0, o1, o2, o3, p0, p1, p2, p3, second_out, base_out, start_out, shares):
    u, v, c, _ = place()

    def run(firsts, seconds):
        panels(u, v, firsts, seconds, second_out, shares=shares)
        taken = jnp.dot(second_out[...], shares[...], preferred_element_type=F32).T
        base = seconds[0][BLOCK:, :].astype(F32) - taken[:R]
        base_out[...] = base
        start_out[...] = base.astype(BF16)

    own, peer = (o0, o1, o2, o3), (p0, p1, p2, p3)

    @pl.when(c == 0)
    def _():
        run(own, peer)

    @pl.when(c != 0)
    def _():
        run(peer, own)


def product_block(o0, o1, o2, o3, p0, p1, p2, p3, second, high_out, low_out, first):
    u, v, c, _ = place()
    own, peer = (o0, o1, o2, o3), (p0, p1, p2, p3)

    @pl.when(c == 0)
    def _():
        panels(u, v, own, (), second, first=first)

    @pl.when(c != 0)
    def _():
        panels(u, v, peer, (), second, first=first)

    total = jnp.dot(second[...], first[...], preferred_element_type=F32)
    high, low = halves(total)
    high_out[...] = high
    low_out[...] = low


def pair_sum(r0, r1, out):
    out[...] = r0[...].astype(F32) + r1[...].astype(F32)


def onward(entry, p_high, p_low, base):
    high, low = halves(entry)
    return base + (nt(high, p_high) + (nt(low, p_high) + nt(high, p_low)))


def hop_block(own, peer, p_high, p_low, base, out):
    out[...] = onward(own[...] + peer[...], p_high[...], p_low[...], base[...]).astype(BF16)


def final_block(*refs):
    entries, (p_high, p_low, base, message, message_peer), outs = refs[:6], refs[6:11], refs[11:]
    _, v, c, _ = place()
    entry = sum(e[...] for e in entries)
    high, low = halves(entry)
    second = onward(entry, p_high[...], p_low[...], base[...])
    first_block = jnp.where(c == 0, message[...], message_peer[...])
    first = first_block[BLOCK:, :].astype(F32) - (nt(high, first_block[:BLOCK, :]) + nt(low, first_block[:BLOCK, :]))
    states = jnp.concatenate([first, second], axis=0)
    for d in range(4):
        at = lax.rem(v + d, 4) * CHIP + c * ROWS
        outs[d][...] = pltpu.roll(states, lax.rem(BLOCK - at, BLOCK), 1)[:, :ROWS]


def hop(out, plane, *beside):
    arrived = []
    for j in range(2):
        def target(y, x, c, z, j=j):
            y, x, c, _ = along_v(3 - j if c else j)(y, x, c, z)
            return (y, x, c, z + 1) if z + 1 == plane else None
        arrived.append(send(out, target))
    arrived, beside = lax.optimization_barrier((arrived, beside))
    own = call(pair_sum, shape((R, BLOCK), F32), *arrived)
    return (own, to_peer(own)), beside


def local(inverses, lower, forcing, inflow):
    forcing = jnp.swapaxes(forcing, 1, 2)
    inflow = inflow.T
    inverses_peer = to_peer(inverses)
    lower_peer = to_peer(lower)
    inv_own = call(inverse_piece, shape((CHIP, N)), inverses, inverses_peer)
    lower_own = call(hold, shape((ROWS, N)), lower)
    piece = shape((CHIP, BLOCK))
    low = call(
        lower_pieces, [piece] * 4, lower_own, lower_peer,
        scratch=[pltpu.VMEM((CHIP, N), BF16), pltpu.VMEM((4, CHIP, BLOCK), BF16)],
    )
    low = [low[0]] + [send(low[d], along_v(d)) for d in range(1, 4)]
    forcing_peer = to_peer(forcing)
    inflow_peer = to_peer(inflow)
    inv_own, low[1] = lax.optimization_barrier((inv_own, low[1]))
    inv_2 = send(inv_own, along_v(2))
    own = call(
        lower_block, shape((BLOCK + R, BLOCK)), *low, forcing, forcing_peer, inflow, inflow_peer,
        scratch=[pltpu.VMEM((CHIP, LANES), F32)],
    )
    inv_own, own = lax.optimization_barrier((inv_own, own))
    inv_3, inv_1 = send(inv_own, along_v(3)), send(inv_own, along_v(1))
    inv = [inv_own, inv_3, inv_2, inv_1]
    panel = around(own, along_u, LOWER_ORDER)

    message = call(
        coupling_block, shape((BLOCK + R, BLOCK)), *inv, *panel,
        scratch=[
            pltpu.VMEM((BLOCK, N), BF16), pltpu.VMEM((N, BLOCK + LANES), BF16), pltpu.VMEM((BLOCK, LANES), BF16),
        ],
        flops=2 * BLOCK * BLOCK * N,
    )
    turn = around(message, across, TURN_ORDER)
    turn_peer = [to_peer(value) for value in turn]
    second, base, out = call(
        base_block, [shape((BLOCK, N)), shape((R, BLOCK), F32), shape((R, BLOCK))], *turn, *turn_peer,
        scratch=[pltpu.VMEM((N, LANES), BF16)],
    )
    p_high, p_low = call(
        product_block, [shape((BLOCK, BLOCK)), shape((BLOCK, BLOCK))], *turn, *turn_peer, second,
        scratch=[pltpu.VMEM((N, BLOCK), BF16)], flops=2 * BLOCK * BLOCK * N,
    )

    entries = []
    for plane in range(1, Z):
        entry, (p_high, p_low) = hop(out, plane, p_high, p_low)
        entries += entry
        if plane + 1 < Z:
            out = call(hop_block, shape((R, BLOCK)), *entry, p_high, p_low, base)
    finals = call(
        final_block, [shape((2 * R, ROWS), F32)] * 4, *entries, p_high, p_low, base, turn[0], turn_peer[0]
    )
    total = finals[0]
    for d in range(1, 4):
        total = total + send(finals[d], along_v(d))
    return jnp.swapaxes(total.reshape(2, R, ROWS), 1, 2)


def solution(mesh):
    placed = (
        P("blk", "group", None),
        P("blk", "group", None),
        P("blk", "group", None),
        P("group", None),
    )
    return jax.shard_map(
        local, mesh=mesh, in_specs=placed, out_specs=P("blk", "group", None), check_vma=False
    )
```

```python
import jax
import jax.numpy as jnp
from jax import lax
from jax.experimental import pallas as pl
from jax.experimental.pallas import tpu as pltpu
from jax.sharding import PartitionSpec as P

Y, X, CORES, Z = 4, 4, 2, 4
AXES = ("group", "blk")
ROWS = 48
CHIP = ROWS * CORES
BLOCK = CHIP * X
N = BLOCK * Y
R = 32
LANES = 128
LOWER_ORDER = (0, 2, 3, 1)
TURN_ORDER = (0, 3, 1, 2)
F32, BF16 = jnp.float32, jnp.bfloat16


def send(value, target):
    pairs = []
    for y in range(Y):
        for x in range(X):
            for c in range(CORES):
                for z in range(Z):
                    to = target(y, x, c, z)
                    if to is not None:
                        ty, tx, tc, tz = to
                        pairs.append((
                            ((y * X + x) * CORES + c) * Z + z,
                            ((ty % Y * X + tx % X) * CORES + tc) * Z + tz,
                        ))
    return lax.ppermute(value, AXES, pairs)


def around(value, along, order):
    return [value] + [send(value, along(d)) for d in order[1:]]


def to_peer(value):
    return send(value, lambda y, x, c, z: (y, x, 1 - c, z))


def along_v(d):
    return lambda y, x, c, z: (y, x + d, c, z) if z % 2 == 0 else (y + d, x, c, z)


def along_u(d):
    return lambda y, x, c, z: (y + d, x, c, z) if z % 2 == 0 else (y, x + d, c, z)


def across(d):
    return lambda y, x, c, z: (along_u(d) if c == 0 else along_v(d))(y, x, c, z)


def place():
    group, z = lax.axis_index("group"), lax.axis_index("blk")
    y, x = group // (X * CORES), (group // CORES) % X
    even = z % 2 == 0
    return jnp.where(even, y, x), jnp.where(even, x, y), group % CORES, z


def chunk(u, v, z):
    return pl.multiple_of(jnp.where(z % 2 == 0, u * BLOCK + v * CHIP, v * BLOCK + u * CHIP), 32)


def rows_at(start, size):
    return pl.ds(pl.multiple_of(start, 16), size)


def lanes_at(start, size):
    return pl.ds(pl.multiple_of(start, 128), size)


def behind(me, d):
    return lax.rem(me - d + 4, 4)


def call(kernel, out, *args, scratch=(), flops=0):
    moved = sum(a.size * a.dtype.itemsize for a in args)
    return pl.pallas_call(
        kernel,
        out_shape=out,
        in_specs=[pl.BlockSpec(memory_space=pltpu.VMEM)] * len(args),
        out_specs=jax.tree.map(lambda _: pl.BlockSpec(memory_space=pltpu.VMEM), out),
        scratch_shapes=list(scratch),
        cost_estimate=pl.CostEstimate(flops=flops, bytes_accessed=moved, transcendentals=0),
        compiler_params=pltpu.CompilerParams(vmem_limit_bytes=24 * 2**20),
    )(*args)


def shape(dims, kind=BF16):
    return jax.ShapeDtypeStruct(dims, kind)


def nt(a, b):
    return lax.dot_general(a, b, (((1,), (1,)), ((), ())), preferred_element_type=F32)


def halves(value):
    high = value.astype(BF16)
    return high, (value - high.astype(F32)).astype(BF16)


def hold(own, out):
    out[...] = own[place()[2]]


def lower_pieces(own, peer, *refs):
    outs, rows, cut = refs[:4], refs[4], refs[5]
    _, v, c, z = place()
    rows[rows_at(c * ROWS, ROWS), :] = own[...]
    rows[rows_at((1 - c) * ROWS, ROWS), :] = peer[c]

    @pl.when(z % 2 == 0)
    def _():
        for b in range(4):
            cut[b] = jnp.concatenate(
                [rows[:, i * BLOCK + b * CHIP:i * BLOCK + (b + 1) * CHIP] for i in range(4)], axis=1
            )

    @pl.when(z % 2 == 1)
    def _():
        for b in range(4):
            cut[b] = rows[:, b * BLOCK:(b + 1) * BLOCK]

    for d in range(4):
        outs[d][...] = cut[lax.rem(v + d, 4)]


def inverse_piece(own, peer, out):
    c = place()[2]
    out[rows_at(c * ROWS, ROWS), :] = own[c]
    out[rows_at((1 - c) * ROWS, ROWS), :] = peer[c]


def lower_block(p0, p1, p2, p3, forcing, forcing_peer, inflow, inflow_peer, out, sides):
    _, v, c, _ = place()
    for d, piece in enumerate((p0, p1, p2, p3)):
        out[rows_at(behind(v, d) * CHIP, CHIP), :] = piece[...]
    for f, e, at in ((forcing, inflow, c * ROWS), (forcing_peer, inflow_peer, (1 - c) * ROWS)):
        high, low = halves(e[...])
        side = jnp.concatenate([f[c].astype(F32), high.astype(F32), low.astype(F32), jnp.zeros((R, ROWS), F32)], axis=0)
        side = jnp.concatenate([side, jnp.zeros((LANES, LANES - ROWS), F32)], axis=1).T
        sides[rows_at(at, ROWS), :] = side[:ROWS]
    for g in range(3):
        out[BLOCK:, g * LANES:(g + 1) * LANES] = sides[g * R:(g + 1) * R, :].astype(BF16)


def coupling_block(a0, a3, a2, a1, l0, l1, l2, l3, out, panel, lower, entry):
    u, v, c, z = place()
    lower[:, BLOCK:] = jnp.zeros((N, LANES), BF16)
    for d, piece in enumerate((a0, a1, a2, a3)):
        panel[rows_at(behind(v, d) * CHIP, CHIP), :] = piece[...]
    for d, piece in zip(LOWER_ORDER, (l0, l1, l2, l3)):
        from_u = behind(u, d)
        for j in range(4):
            lower[rows_at(chunk(from_u, j, z), CHIP), :BLOCK] = piece[j * CHIP:(j + 1) * CHIP, :]
        at = chunk(from_u, v, z)
        for g in range(3):
            part = piece[BLOCK:, g * LANES:(g + 1) * LANES]
            lower[rows_at(at + g * R, R), BLOCK:] = part
            entry[rows_at(from_u * CHIP + g * R, R), :] = part
    both = jnp.dot(panel[...], lower[...], preferred_element_type=F32)
    block = both[:, :BLOCK].astype(BF16)
    share = both[:, BLOCK:BLOCK + R]
    known = jnp.dot(block, entry[...], preferred_element_type=F32)
    known = known[:, R:2 * R] + known[:, 2 * R:3 * R]
    share = share - jnp.where((z == 0) & (c == 0), known, 0.0)
    share = jnp.concatenate([share, jnp.zeros((BLOCK, LANES - R), F32)], axis=1).T[:R]
    out[:BLOCK, :] = block
    out[BLOCK:, :] = share.astype(BF16)


def panels(u, v, firsts, seconds, second, first=None, shares=None):
    for d, piece in zip(TURN_ORDER, seconds):
        second[:, lanes_at(behind(v, d) * BLOCK, BLOCK)] = piece[:BLOCK, :]
    for d, piece in zip(TURN_ORDER, firsts):
        from_u = behind(u, d)
        if shares is not None:
            side = piece[BLOCK:, :].astype(F32)
            side = jnp.concatenate([side, jnp.zeros((LANES - R, BLOCK), F32)], axis=0).T.astype(BF16)
        for j in range(4):
            at = rows_at(j * BLOCK + from_u * CHIP, CHIP)
            if first is not None:
                first[at, :] = piece[j * CHIP:(j + 1) * CHIP, :]
            if shares is not None:
                shares[at, :] = side[j * CHIP:(j + 1) * CHIP, :]


def base_block(o0, o1, o2, o3, p0, p1, p2, p3, second_out, base_out, start_out, shares):
    u, v, c, _ = place()

    def run(firsts, seconds):
        panels(u, v, firsts, seconds, second_out, shares=shares)
        taken = jnp.dot(second_out[...], shares[...], preferred_element_type=F32).T
        base = seconds[0][BLOCK:, :].astype(F32) - taken[:R]
        base_out[...] = base
        start_out[...] = base.astype(BF16)

    own, peer = (o0, o1, o2, o3), (p0, p1, p2, p3)

    @pl.when(c == 0)
    def _():
        run(own, peer)

    @pl.when(c != 0)
    def _():
        run(peer, own)


def product_block(o0, o1, o2, o3, p0, p1, p2, p3, second, high_out, low_out, first):
    u, v, c, _ = place()
    own, peer = (o0, o1, o2, o3), (p0, p1, p2, p3)

    @pl.when(c == 0)
    def _():
        panels(u, v, own, (), second, first=first)

    @pl.when(c != 0)
    def _():
        panels(u, v, peer, (), second, first=first)

    total = jnp.dot(second[...], first[...], preferred_element_type=F32)
    high, low = halves(total)
    high_out[...] = high
    low_out[...] = low


def pair_sum(r0, r1, out):
    out[...] = r0[...].astype(F32) + r1[...].astype(F32)


def onward(entry, p_high, p_low, base):
    high, low = halves(entry)
    return base + (nt(high, p_high) + (nt(low, p_high) + nt(high, p_low)))


def hop_block(own, peer, p_high, p_low, base, out):
    out[...] = onward(own[...] + peer[...], p_high[...], p_low[...], base[...]).astype(BF16)


def final_block(*refs):
    entries, (p_high, p_low, base, message, message_peer), outs = refs[:6], refs[6:11], refs[11:]
    _, v, c, _ = place()
    entry = sum(e[...] for e in entries)
    high, low = halves(entry)
    second = onward(entry, p_high[...], p_low[...], base[...])
    first_block = jnp.where(c == 0, message[...], message_peer[...])
    first = first_block[BLOCK:, :].astype(F32) - (nt(high, first_block[:BLOCK, :]) + nt(low, first_block[:BLOCK, :]))
    states = jnp.concatenate([first, second], axis=0)
    for d in range(4):
        at = lax.rem(v + d, 4) * CHIP + c * ROWS
        outs[d][...] = pltpu.roll(states, lax.rem(BLOCK - at, BLOCK), 1)[:, :ROWS]


def hop(out, plane, *beside):
    arrived = []
    for j in range(2):
        def target(y, x, c, z, j=j):
            y, x, c, _ = along_v(3 - j if c else j)(y, x, c, z)
            return (y, x, c, z + 1) if z + 1 == plane else None
        arrived.append(send(out, target))
    arrived, beside = lax.optimization_barrier((arrived, beside))
    own = call(pair_sum, shape((R, BLOCK), F32), *arrived)
    return (own, to_peer(own)), beside


def local(inverses, lower, forcing, inflow):
    forcing = jnp.swapaxes(forcing, 1, 2)
    inflow = inflow.T
    inverses_peer = to_peer(inverses)
    lower_peer = to_peer(lower)
    inv_own = call(inverse_piece, shape((CHIP, N)), inverses, inverses_peer)
    lower_own = call(hold, shape((ROWS, N)), lower)
    piece = shape((CHIP, BLOCK))
    low = call(
        lower_pieces, [piece] * 4, lower_own, lower_peer,
        scratch=[pltpu.VMEM((CHIP, N), BF16), pltpu.VMEM((4, CHIP, BLOCK), BF16)],
    )
    low = [low[0]] + [send(low[d], along_v(d)) for d in range(1, 4)]
    forcing_peer = to_peer(forcing)
    inflow_peer = to_peer(inflow)
    inv_own, low[1] = lax.optimization_barrier((inv_own, low[1]))
    inv_2 = send(inv_own, along_v(2))
    own = call(
        lower_block, shape((BLOCK + R, BLOCK)), *low, forcing, forcing_peer, inflow, inflow_peer,
        scratch=[pltpu.VMEM((CHIP, LANES), F32)],
    )
    inv_own, own = lax.optimization_barrier((inv_own, own))
    inv_3, inv_1 = send(inv_own, along_v(3)), send(inv_own, along_v(1))
    inv = [inv_own, inv_3, inv_2, inv_1]
    panel = around(own, along_u, LOWER_ORDER)

    message = call(
        coupling_block, shape((BLOCK + R, BLOCK)), *inv, *panel,
        scratch=[
            pltpu.VMEM((BLOCK, N), BF16), pltpu.VMEM((N, BLOCK + LANES), BF16), pltpu.VMEM((BLOCK, LANES), BF16),
        ],
        flops=2 * BLOCK * BLOCK * N,
    )
    turn = around(message, across, TURN_ORDER)
    turn_peer = [to_peer(value) for value in turn]
    second, base, out = call(
        base_block, [shape((BLOCK, N)), shape((R, BLOCK), F32), shape((R, BLOCK))], *turn, *turn_peer,
        scratch=[pltpu.VMEM((N, LANES), BF16)],
    )
    p_high, p_low = call(
        product_block, [shape((BLOCK, BLOCK)), shape((BLOCK, BLOCK))], *turn, *turn_peer, second,
        scratch=[pltpu.VMEM((N, BLOCK), BF16)], flops=2 * BLOCK * BLOCK * N,
    )

    entries = []
    for plane in range(1, Z):
        entry, (p_high, p_low) = hop(out, plane, p_high, p_low)
        entries += entry
        if plane + 1 < Z:
            out = call(hop_block, shape((R, BLOCK)), *entry, p_high, p_low, base)
    finals = call(
        final_block, [shape((2 * R, ROWS), F32)] * 4, *entries, p_high, p_low, base, turn[0], turn_peer[0]
    )
    total = finals[0]
    for d in range(1, 4):
        total = total + send(finals[d], along_v(d))
    return jnp.swapaxes(total.reshape(2, R, ROWS), 1, 2)


def solution(mesh):
    placed = (
        P("blk", "group", None),
        P("blk", "group", None),
        P("blk", "group", None),
        P("group", None),
    )
    return jax.shard_map(
        local, mesh=mesh, in_specs=placed, out_specs=P("blk", "group", None), check_vma=False
    )
```

```python
import jax
import jax.numpy as jnp
from jax import lax
from jax.experimental import pallas as pl
from jax.experimental.pallas import tpu as pltpu
from jax.sharding import PartitionSpec as P

Y, X, CORES, Z = 4, 4, 2, 4
AXES = ("group", "blk")
ROWS = 48
CHIP = ROWS * CORES
BLOCK = CHIP * X
N = BLOCK * Y
R = 32
LANES = 128
LOWER_ORDER = (0, 2, 3, 1)
TURN_ORDER = (0, 3, 1, 2)
F32, BF16 = jnp.float32, jnp.bfloat16


def send(value, target):
    pairs = []
    for y in range(Y):
        for x in range(X):
            for c in range(CORES):
                for z in range(Z):
                    to = target(y, x, c, z)
                    if to is not None:
                        ty, tx, tc, tz = to
                        pairs.append((
                            ((y * X + x) * CORES + c) * Z + z,
                            ((ty % Y * X + tx % X) * CORES + tc) * Z + tz,
                        ))
    return lax.ppermute(value, AXES, pairs)


def around(value, along, order):
    return [value] + [send(value, along(d)) for d in order[1:]]


def to_peer(value):
    return send(value, lambda y, x, c, z: (y, x, 1 - c, z))


def along_v(d):
    return lambda y, x, c, z: (y, x + d, c, z) if z % 2 == 0 else (y + d, x, c, z)


def along_u(d):
    return lambda y, x, c, z: (y + d, x, c, z) if z % 2 == 0 else (y, x + d, c, z)


def across(d):
    return lambda y, x, c, z: (along_u(d) if c == 0 else along_v(d))(y, x, c, z)


def place():
    group, z = lax.axis_index("group"), lax.axis_index("blk")
    y, x = group // (X * CORES), (group // CORES) % X
    even = z % 2 == 0
    return jnp.where(even, y, x), jnp.where(even, x, y), group % CORES, z


def chunk(u, v, z):
    return pl.multiple_of(jnp.where(z % 2 == 0, u * BLOCK + v * CHIP, v * BLOCK + u * CHIP), 32)


def rows_at(start, size):
    return pl.ds(pl.multiple_of(start, 16), size)


def lanes_at(start, size):
    return pl.ds(pl.multiple_of(start, 128), size)


def behind(me, d):
    return lax.rem(me - d + 4, 4)


def call(kernel, out, *args, scratch=(), flops=0):
    moved = sum(a.size * a.dtype.itemsize for a in args)
    return pl.pallas_call(
        kernel,
        out_shape=out,
        in_specs=[pl.BlockSpec(memory_space=pltpu.VMEM)] * len(args),
        out_specs=jax.tree.map(lambda _: pl.BlockSpec(memory_space=pltpu.VMEM), out),
        scratch_shapes=list(scratch),
        cost_estimate=pl.CostEstimate(flops=flops, bytes_accessed=moved, transcendentals=0),
        compiler_params=pltpu.CompilerParams(vmem_limit_bytes=24 * 2**20),
    )(*args)


def shape(dims, kind=BF16):
    return jax.ShapeDtypeStruct(dims, kind)


def nt(a, b):
    return lax.dot_general(a, b, (((1,), (1,)), ((), ())), preferred_element_type=F32)


def halves(value):
    high = value.astype(BF16)
    return high, (value - high.astype(F32)).astype(BF16)


def hold(own, out):
    out[...] = own[place()[2]]


def lower_pieces(own, peer, *refs):
    outs, rows, cut = refs[:4], refs[4], refs[5]
    _, v, c, z = place()
    rows[rows_at(c * ROWS, ROWS), :] = own[...]
    rows[rows_at((1 - c) * ROWS, ROWS), :] = peer[c]

    @pl.when(z % 2 == 0)
    def _():
        for b in range(4):
            cut[b] = jnp.concatenate(
                [rows[:, i * BLOCK + b * CHIP:i * BLOCK + (b + 1) * CHIP] for i in range(4)], axis=1
            )

    @pl.when(z % 2 == 1)
    def _():
        for b in range(4):
            cut[b] = rows[:, b * BLOCK:(b + 1) * BLOCK]

    for d in range(4):
        outs[d][...] = cut[lax.rem(v + d, 4)]


def inverse_piece(own, peer, out):
    c = place()[2]
    out[rows_at(c * ROWS, ROWS), :] = own[c]
    out[rows_at((1 - c) * ROWS, ROWS), :] = peer[c]


def lower_block(p0, p1, p2, p3, forcing, forcing_peer, inflow, inflow_peer, out, sides):
    _, v, c, _ = place()
    for d, piece in enumerate((p0, p1, p2, p3)):
        out[rows_at(behind(v, d) * CHIP, CHIP), :] = piece[...]
    for f, e, at in ((forcing, inflow, c * ROWS), (forcing_peer, inflow_peer, (1 - c) * ROWS)):
        high, low = halves(e[...])
        side = jnp.concatenate([f[c].astype(F32), high.astype(F32), low.astype(F32), jnp.zeros((R, ROWS), F32)], axis=0)
        side = jnp.concatenate([side, jnp.zeros((LANES, LANES - ROWS), F32)], axis=1).T
        sides[rows_at(at, ROWS), :] = side[:ROWS]
    for g in range(3):
        out[BLOCK:, g * LANES:(g + 1) * LANES] = sides[g * R:(g + 1) * R, :].astype(BF16)


def coupling_block(a0, a3, a2, a1, l0, l1, l2, l3, out, panel, lower, entry):
    u, v, c, z = place()
    lower[:, BLOCK:] = jnp.zeros((N, LANES), BF16)
    for d, piece in enumerate((a0, a1, a2, a3)):
        panel[rows_at(behind(v, d) * CHIP, CHIP), :] = piece[...]
    for d, piece in zip(LOWER_ORDER, (l0, l1, l2, l3)):
        from_u = behind(u, d)
        for j in range(4):
            lower[rows_at(chunk(from_u, j, z), CHIP), :BLOCK] = piece[j * CHIP:(j + 1) * CHIP, :]
        at = chunk(from_u, v, z)
        for g in range(3):
            part = piece[BLOCK:, g * LANES:(g + 1) * LANES]
            lower[rows_at(at + g * R, R), BLOCK:] = part
            entry[rows_at(from_u * CHIP + g * R, R), :] = part
    both = jnp.dot(panel[...], lower[...], preferred_element_type=F32)
    block = both[:, :BLOCK].astype(BF16)
    share = both[:, BLOCK:BLOCK + R]
    known = jnp.dot(block, entry[...], preferred_element_type=F32)
    known = known[:, R:2 * R] + known[:, 2 * R:3 * R]
    share = share - jnp.where((z == 0) & (c == 0), known, 0.0)
    share = jnp.concatenate([share, jnp.zeros((BLOCK, LANES - R), F32)], axis=1).T[:R]
    out[:BLOCK, :] = block
    out[BLOCK:, :] = share.astype(BF16)


def panels(u, v, firsts, seconds, second, first=None, shares=None):
    for d, piece in zip(TURN_ORDER, seconds):
        second[:, lanes_at(behind(v, d) * BLOCK, BLOCK)] = piece[:BLOCK, :]
    for d, piece in zip(TURN_ORDER, firsts):
        from_u = behind(u, d)
        if shares is not None:
            side = piece[BLOCK:, :].astype(F32)
            side = jnp.concatenate([side, jnp.zeros((LANES - R, BLOCK), F32)], axis=0).T.astype(BF16)
        for j in range(4):
            at = rows_at(j * BLOCK + from_u * CHIP, CHIP)
            if first is not None:
                first[at, :] = piece[j * CHIP:(j + 1) * CHIP, :]
            if shares is not None:
                shares[at, :] = side[j * CHIP:(j + 1) * CHIP, :]


def base_block(o0, o1, o2, o3, p0, p1, p2, p3, second_out, base_out, start_out, shares):
    u, v, c, _ = place()

    def run(firsts, seconds):
        panels(u, v, firsts, seconds, second_out, shares=shares)
        taken = jnp.dot(second_out[...], shares[...], preferred_element_type=F32).T
        base = seconds[0][BLOCK:, :].astype(F32) - taken[:R]
        base_out[...] = base
        start_out[...] = base.astype(BF16)

    own, peer = (o0, o1, o2, o3), (p0, p1, p2, p3)

    @pl.when(c == 0)
    def _():
        run(own, peer)

    @pl.when(c != 0)
    def _():
        run(peer, own)


def product_block(o0, o1, o2, o3, p0, p1, p2, p3, second, high_out, low_out, first):
    u, v, c, _ = place()
    own, peer = (o0, o1, o2, o3), (p0, p1, p2, p3)

    @pl.when(c == 0)
    def _():
        panels(u, v, own, (), second, first=first)

    @pl.when(c != 0)
    def _():
        panels(u, v, peer, (), second, first=first)

    total = jnp.dot(second[...], first[...], preferred_element_type=F32)
    high, low = halves(total)
    high_out[...] = high
    low_out[...] = low


def pair_sum(r0, r1, out, sent):
    total = r0[...].astype(F32) + r1[...].astype(F32)
    out[...] = total
    sent[...] = total.astype(BF16)


def onward(entry, p_high, p_low, base):
    high, low = halves(entry)
    return base + (nt(high, p_high) + (nt(low, p_high) + nt(high, p_low)))


def hop_block(own, peer, p_high, p_low, base, out):
    out[...] = onward(own[...] + peer[...], p_high[...], p_low[...], base[...]).astype(BF16)


def final_block(*refs):
    entries, (p_high, p_low, base, message, message_peer), outs = refs[:6], refs[6:11], refs[11:]
    _, v, c, _ = place()
    entry = sum(e[...] for e in entries)
    high, low = halves(entry)
    second = onward(entry, p_high[...], p_low[...], base[...])
    first_block = jnp.where(c == 0, message[...], message_peer[...])
    first = first_block[BLOCK:, :].astype(F32) - (nt(high, first_block[:BLOCK, :]) + nt(low, first_block[:BLOCK, :]))
    states = jnp.concatenate([first, second], axis=0)
    for d in range(4):
        at = lax.rem(v + d, 4) * CHIP + c * ROWS
        outs[d][...] = pltpu.roll(states, lax.rem(BLOCK - at, BLOCK), 1)[:, :ROWS]


def hop(out, plane, *beside):
    arrived = []
    for j in range(2):
        def target(y, x, c, z, j=j):
            y, x, c, _ = along_v(3 - j if c else j)(y, x, c, z)
            return (y, x, c, z + 1) if z + 1 == plane else None
        arrived.append(send(out, target))
    arrived, beside = lax.optimization_barrier((arrived, beside))
    own, sent = call(pair_sum, [shape((R, BLOCK), F32), shape((R, BLOCK))], *arrived)
    return (own, to_peer(sent)), beside


def local(inverses, lower, forcing, inflow):
    forcing = jnp.swapaxes(forcing, 1, 2)
    inflow = inflow.T
    inverses_peer = to_peer(inverses)
    lower_peer = to_peer(lower)
    inv_own = call(inverse_piece, shape((CHIP, N)), inverses, inverses_peer)
    lower_own = call(hold, shape((ROWS, N)), lower)
    piece = shape((CHIP, BLOCK))
    low = call(
        lower_pieces, [piece] * 4, lower_own, lower_peer,
        scratch=[pltpu.VMEM((CHIP, N), BF16), pltpu.VMEM((4, CHIP, BLOCK), BF16)],
    )
    low = [low[0]] + [send(low[d], along_v(d)) for d in range(1, 4)]
    forcing_peer = to_peer(forcing)
    inflow_peer = to_peer(inflow)
    inv_own, low[1] = lax.optimization_barrier((inv_own, low[1]))
    inv_2 = send(inv_own, along_v(2))
    own = call(
        lower_block, shape((BLOCK + R, BLOCK)), *low, forcing, forcing_peer, inflow, inflow_peer,
        scratch=[pltpu.VMEM((CHIP, LANES), F32)],
    )
    inv_own, own = lax.optimization_barrier((inv_own, own))
    inv_3, inv_1 = send(inv_own, along_v(3)), send(inv_own, along_v(1))
    inv = [inv_own, inv_3, inv_2, inv_1]
    panel = around(own, along_u, LOWER_ORDER)

    message = call(
        coupling_block, shape((BLOCK + R, BLOCK)), *inv, *panel,
        scratch=[
            pltpu.VMEM((BLOCK, N), BF16), pltpu.VMEM((N, BLOCK + LANES), BF16), pltpu.VMEM((BLOCK, LANES), BF16),
        ],
        flops=2 * BLOCK * BLOCK * N,
    )
    turn = around(message, across, TURN_ORDER)
    turn_peer = [to_peer(value) for value in turn]
    second, base, out = call(
        base_block, [shape((BLOCK, N)), shape((R, BLOCK), F32), shape((R, BLOCK))], *turn, *turn_peer,
        scratch=[pltpu.VMEM((N, LANES), BF16)],
    )
    p_high, p_low = call(
        product_block, [shape((BLOCK, BLOCK)), shape((BLOCK, BLOCK))], *turn, *turn_peer, second,
        scratch=[pltpu.VMEM((N, BLOCK), BF16)], flops=2 * BLOCK * BLOCK * N,
    )

    entries = []
    for plane in range(1, Z):
        entry, (p_high, p_low) = hop(out, plane, p_high, p_low)
        entries += entry
        if plane + 1 < Z:
            out = call(hop_block, shape((R, BLOCK)), *entry, p_high, p_low, base)
    finals = call(
        final_block, [shape((2 * R, ROWS), F32)] * 4, *entries, p_high, p_low, base, turn[0], turn_peer[0]
    )
    total = finals[0]
    for d in range(1, 4):
        total = total + send(finals[d], along_v(d))
    return jnp.swapaxes(total.reshape(2, R, ROWS), 1, 2)


def solution(mesh):
    placed = (
        P("blk", "group", None),
        P("blk", "group", None),
        P("blk", "group", None),
        P("group", None),
    )
    return jax.shard_map(
        local, mesh=mesh, in_specs=placed, out_specs=P("blk", "group", None), check_vma=False
    )
```
